256 devices in a mesh: seq: 64 (over y_lo, z, x), chan: 4 (over y_hi, core).
Axes of the slice: x: 4, y: 4 (y_hi: 2, y_lo: 2; y = y_hi * 2 + y_lo), z: 8, core: 2. Of those that a mesh axis runs over, the one named last changes fastest.
Arguments:
- features: bfloat16 [16384, 4096], P('seq', 'chan'), may hold values from -6 to 6
- w_in: bfloat16 [4096, 3, 2048], P('seq', None, 'chan'), may hold values from -0.09375 to 0.09375
- filter_real: float32 [16384, 2048], P('seq', 'chan'), may hold values from -6 to 6
- filter_imag: float32 [16384, 2048], P('seq', 'chan'), may hold values from -6 to 6
- skip_gain: float32 [2048], P('chan'), may hold values from -4 to 4
Outputs:
- gated_output: bfloat16 [16384, 2048], P('seq', 'chan')
The draws below stay inside these ranges and needn't reach their ends.
All inputs are finite; a program needn't handle non-finite values.
Results may differ from the reference program's by a relative error of at most 0.0064.
Values may be sent and summed in bfloat16 or wider, within the bound.
A program may use at most 128 MiB of HBM per device.

```python
import jax
import jax.numpy as jnp
from jax import lax

D = 4096
CH = 2048
LENGTH = 16384


def level_of(key, extent, split, smallest, largest):
    gain, own = 1.0, jax.random.fold_in(key, 6)
    for position, blocks in split:
        draws = jnp.exp(jax.random.uniform(jax.random.fold_in(own, position), (blocks,), jnp.float32, smallest / len(split), largest / len(split)))
        gain = gain * jnp.repeat(draws, extent[position] // blocks).reshape([-1 if axis == position else 1 for axis in range(len(extent))])
    return gain


def scatter_about(own_key, extent, width, bound, shards=(), held_as=jnp.bfloat16):
    array = width * jax.random.normal(own_key, extent, jnp.float32)
    if shards:
        array = array * level_of(own_key, extent, shards, -0.22, 0.18)
    return jnp.clip(array, -bound, bound).astype(held_as)


def setup_inputs(seed: int = 0) -> dict:
    seeds = jax.random.split(jax.random.key(seed), 6)
    return {
        "features": scatter_about(seeds[0], (LENGTH, D), 1.0, 6.0, ((0, 64), (1, 4))),
        "w_in": scatter_about(seeds[1], (D, 3, CH), D ** -0.5, 0.09375, ((0, 64), (2, 4))),
        "filter_real": scatter_about(seeds[2], (LENGTH, CH), 1.0, 6.0, ((0, 64), (1, 4)), jnp.float32),
        "filter_imag": scatter_about(seeds[3], (LENGTH, CH), 1.0, 6.0, ((0, 64), (1, 4)), jnp.float32),
        "skip_gain": scatter_about(seeds[4], (CH,), 1.0, 4.0, ((0, 4),), jnp.float32),
    }


def reference(features, w_in, filter_real, filter_imag, skip_gain):
    input_gate = jnp.dot(features, w_in[:, 0, :], preferred_element_type=jnp.float32).astype(jnp.bfloat16)
    value_stream = jnp.dot(features, w_in[:, 1, :], preferred_element_type=jnp.float32).astype(jnp.bfloat16)
    output_gate = jnp.dot(features, w_in[:, 2, :], preferred_element_type=jnp.float32).astype(jnp.bfloat16)
    signal = input_gate.astype(jnp.float32) * value_stream.astype(jnp.float32)
    spectrum = jnp.fft.fft(signal, axis=0)
    filtered = lax.complex(filter_real, filter_imag) * spectrum
    convolved = jnp.real(jnp.fft.ifft(filtered, axis=0))
    result = output_gate.astype(jnp.float32) * (convolved + skip_gain[None, :] * signal)
    return result.astype(jnp.bfloat16)
```

```python
import functools

import jax
import jax.numpy as jnp
import numpy as np
from jax import lax
from jax.experimental import pallas as pl
from jax.experimental.pallas import tpu as pltpu
from jax.sharding import Mesh
from jax.sharding import PartitionSpec as P

MESH = pl.DeviceIdType.MESH
F32 = jnp.float32
BF16 = jnp.bfloat16

YL, NZ, NX, YH, NC = 2, 8, 4, 2, 2
NS = YL * NZ * NX
Q = YL * NZ
ROWS = 256
HALF = ROWS // 2
DBLK = 1024
LANES = 128
CB = 8
N1 = 128
WROWS = 64 * NX
COLS = 3 * LANES


def split16(table):
    high = table.astype(BF16)
    return high, (table - high.astype(F32)).astype(BF16)


def tables():
    index = np.arange(N1)
    angle = 2.0 * np.pi * ((index[:, None] * index[None, :]) % N1) / N1
    cos, sin = np.cos(angle), np.sin(angle)
    twist = 2.0 * np.pi * (index[:, None] * index[None, :]) / (N1 * N1)

    def pair(table):
        high = table.astype(np.float32).astype(jnp.bfloat16)
        low = (table - high.astype(np.float64)).astype(np.float32).astype(jnp.bfloat16)
        return high, low

    first = pair(np.concatenate([cos, -sin], 0))
    first = np.concatenate(first, 1)
    forward = np.concatenate(pair(np.block([[cos, sin], [-sin, cos]])), 0)
    back = np.concatenate(pair(np.block([[cos, -sin], [sin, cos]])), 0)
    last = np.concatenate(pair(np.concatenate([cos, -sin], 1) / (N1 * N1)), 0)
    return (
        first,
        forward,
        back,
        last,
        np.cos(twist).astype(np.float32),
        np.sin(twist).astype(np.float32),
    )


def dot(a, b):
    return jnp.dot(a, b, preferred_element_type=F32)


def dot_nt(a, b):
    return lax.dot_general(a, b, (((1,), (1,)), ((), ())), preferred_element_type=F32)


def three_pass(product, stacked, value):
    m = stacked.shape[0] // 2
    high, low = split16(value)
    both = product(stacked, high)
    return both[:m] + both[m:] + product(stacked[:m], low)


def kernel(
    feat_ref,
    w_ref,
    fre_ref,
    fim_ref,
    skip_ref,
    first_ref,
    forward_ref,
    back_ref,
    last_ref,
    tc_ref,
    ts_ref,
    out_ref,
    feat,
    wbuf,
    hmsg,
    hbuf,
    sigmsg,
    xs,
    gmsg,
    gbuf,
    ybf,
    ybuf,
    xf,
    yf,
    hre,
    him,
    f_send,
    f_recv,
    w_send,
    ws_recv,
    w_recv,
    g_send,
    g_recv,
    bulk_send,
    bulk_recv,
    local_sem,
):
    yl = lax.axis_index("y_lo")
    z = lax.axis_index("z")
    x = lax.axis_index("x")
    yh = lax.axis_index("y_hi")
    core = lax.axis_index("core")
    q = yl * NZ + z
    me_s = q * NX + x
    me_m = x * Q + q

    def wrap(value, count):
        return lax.rem(value + count, count)

    def at_x(step):
        return {"x": wrap(x + step, NX)}

    def at_z(step):
        return {"z": wrap(z + step, NZ)}

    over_yl, over_yh, over_core = {"y_lo": 1 - yl}, {"y_hi": 1 - yh}, {"core": 1 - core}

    def peer(step):
        m = lax.rem(me_m + step, NS)
        px, pq = m // Q, lax.rem(m, Q)
        return m, pq * NX + px, {"x": px, "y_lo": pq // NZ, "z": lax.rem(pq, NZ)}

    barrier = pltpu.get_barrier_semaphore()

    def greet(step, carry):
        _, _, where = peer(step)
        pl.semaphore_signal(barrier, inc=1, device_id=where, device_id_type=MESH)
        return carry

    lax.fori_loop(1, NS, greet, 0)
    pl.semaphore_signal(barrier, inc=1, device_id=over_yh, device_id_type=MESH)
    pl.semaphore_signal(barrier, inc=1, device_id=over_core, device_id_type=MESH)
    pl.semaphore_wait(barrier, NS + 1)

    started = []

    def w_block(dz, dyl):
        return wbuf.at[(yl if dyl == 0 else 1 - yl) * NZ + wrap(z + dz, NZ)]

    def w_go(src, dst, recv_sem, where):
        index = len([1 for kind, _ in started if kind == "w"])
        copy = pltpu.make_async_remote_copy(
            src_ref=src,
            dst_ref=dst,
            send_sem=w_send.at[index],
            recv_sem=recv_sem,
            device_id=where,
            device_id_type=MESH,
        )
        copy.start()
        started.append(("w", copy))

    def w_await(dst, recv_sem):
        pltpu.make_async_remote_copy(
            src_ref=dst,
            dst_ref=dst,
            send_sem=w_send.at[0],
            recv_sem=recv_sem,
            device_id=over_core,
            device_id_type=MESH,
        ).wait_recv()

    def w_slot(dx):
        return wbuf.at[q, pl.ds(pl.multiple_of(wrap(x + dx, NX) * 64, 64), 64)]

    own_w = pltpu.make_async_copy(w_ref.at[x], w_slot(0), local_sem.at[0])
    own_w.start()
    for step in (1, 3, 2):
        w_go(w_ref.at[wrap(x + step, NX)], w_slot(0), ws_recv.at[3 - step], at_x(step))

    def f_block(dx, dyh, dc, h):
        column = (yh if dyh == 0 else 1 - yh) * NC + (core if dc == 0 else 1 - core)
        return feat.at[wrap(x + dx, NX), column, pl.ds(h * HALF, HALF)]

    def f_sem(dx, dyh, dc, h):
        return f_recv.at[((dx % NX * 2 + dyh) * 2 + dc) * 2 + h]

    def f_go(src, block, here, where):
        dx, dyh, dc, h = here
        index = len([1 for kind, _ in started if kind == "f"])
        copy = pltpu.make_async_remote_copy(
            src_ref=src,
            dst_ref=block,
            send_sem=f_send.at[index],
            recv_sem=f_sem(dx, dyh, dc, h),
            device_id=where,
            device_id_type=MESH,
        )
        copy.start()
        started.append(("f", copy))

    def f_await(dx, dyh, dc, h):
        block = f_block(dx, dyh, dc, h)
        pltpu.make_async_remote_copy(
            src_ref=block,
            dst_ref=block,
            send_sem=f_send.at[0],
            recv_sem=f_sem(dx, dyh, dc, h),
            device_id=over_core,
            device_id_type=MESH,
        ).wait_recv()

    for h in range(2):
        src = feat_ref.at[pl.ds(h * HALF, HALF)]
        block = f_block(0, 0, 0, h)
        f_go(src, block, (3, 0, 0, h), at_x(1))
        f_go(src, block, (1, 0, 0, h), at_x(-1))
        f_go(src, block, (0, 1, 0, h), over_yh)
        f_go(src, block, (0, 0, 1, h), over_core)
    own_f = pltpu.make_async_copy(feat_ref, feat.at[x, yh * NC + core], local_sem.at[1])
    own_f.start()

    def forward_f(dx, dyh, h):
        f_await(dx, dyh, 0, h)
        block = f_block(dx, dyh, 0, h)
        if dx == 0:
            f_go(block, block, (3, dyh, 0, h), at_x(1))
            f_go(block, block, (1, dyh, 0, h), at_x(-1))
        if dx == 3 and h == 0:
            f_go(block, block, (2, dyh, 0, h), at_x(1))
        if dx == 1 and h == 1:
            f_go(block, block, (2, dyh, 0, h), at_x(-1))
        f_go(block, block, (dx, dyh, 1, h), over_core)

    def w_sem(dz, dyl):
        return w_recv.at[dz % NZ * 2 + dyl]

    def forward_w(dz, dyl):
        block = w_block(dz, dyl)
        if (dz, dyl) == (0, 0):
            own_w.wait()
            for step in range(3):
                w_await(w_slot(1 + step), ws_recv.at[step])
            w_go(block, block, w_sem(0, 1), over_yl)
        else:
            w_await(block, w_sem(dz, dyl))
        if -3 < dz <= 0 or (dz == -3 and dyl == 0):
            w_go(block, block, w_sem(dz - 1, dyl), at_z(1))
        if 0 <= dz < 3 or (dz == 3 and dyl == 1):
            w_go(block, block, w_sem(dz + 1, dyl), at_z(-1))

    def filter_rows(part, ref, chunk):
        lanes = pl.ds(pl.multiple_of(chunk * LANES, LANES), LANES)
        block = ref[:, lanes]
        if part == 0:
            block = block + skip_ref[:, lanes]
        turned = block.T
        parts = [turned[:, i * N1 : (i + 1) * N1].reshape(Q, 1, CB, N1) for i in range(2)]
        stacked = jnp.concatenate(parts, 1).reshape(Q, 2 * CB, N1)
        hmsg[pl.ds(chunk * Q, Q), part] = stacked.astype(BF16)

    def filter_chunk(chunk, carry):
        filter_rows(0, fre_ref, chunk)
        filter_rows(1, fim_ref, chunk)
        return carry

    forward_w(0, 0)
    lax.fori_loop(0, NX, filter_chunk, 0)
    forward_w(0, 1)
    own_rows = pl.ds(pl.multiple_of(me_s * 2 * CB, 2 * CB), 2 * CB)

    def h_copy(m, where):
        return pltpu.make_async_remote_copy(
            src_ref=hmsg.at[m],
            dst_ref=hbuf.at[:, own_rows],
            send_sem=bulk_send.at[0],
            recv_sem=bulk_recv.at[0],
            device_id=where,
            device_id_type=MESH,
        )

    def send_h(step, carry):
        m, _, where = peer(step)
        h_copy(m, where).start()
        return carry

    lax.fori_loop(1, NS, send_h, 0)
    own_h = pltpu.make_async_copy(hmsg.at[me_m], hbuf.at[:, own_rows], local_sem.at[2])
    own_h.start()

    for dx in (3, 1):
        forward_f(dx, 0, 0)
    for dz in (-1, 1):
        forward_w(dz, 0)
    for dx in (3, 1):
        forward_f(dx, 0, 1)
    for dz in (-1, 1):
        forward_w(dz, 1)
    forward_f(0, 1, 0)
    for dyl in (0, 1):
        for dz in (-2, 2):
            forward_w(dz, dyl)
    forward_f(0, 1, 1)
    for h in (0, 1):
        for dx in (3, 1):
            forward_f(dx, 1, h)
    for dyl in (0, 1):
        for dz in (-3, 3):
            forward_w(dz, dyl)
    for dyh in (0, 1):
        for h in (0, 1):
            forward_f(2, dyh, h)
    w_await(w_block(-4, 0), w_sem(-4, 0))
    w_await(w_block(4, 1), w_sem(4, 1))
    own_f.wait()
    for dyh in (0, 1):
        for dx in range(NX):
            for h in range(2):
                f_await(dx, dyh, 1, h)

    def project(chunk, carry):
        total = dot(feat[chunk, 0], wbuf[0:4].reshape(DBLK, COLS))
        for j in range(1, 4):
            total = total + dot(feat[chunk, j], wbuf[4 * j : 4 * j + 4].reshape(DBLK, COLS))
        rounded = total.astype(BF16)
        signal = rounded[:, :LANES].astype(F32) * rounded[:, LANES : 2 * LANES].astype(F32)
        gmsg[chunk] = rounded[:, 2 * LANES :]
        turned = signal.T
        parts = [turned[:, i * N1 : (i + 1) * N1].reshape(Q, 1, CB, N1) for i in range(2)]
        stacked = jnp.concatenate(parts, 1).reshape(Q, 2 * CB, N1)
        sigmsg[:, pl.ds(pl.multiple_of(chunk * 16, 16), 16)] = stacked.astype(BF16)
        return carry

    lax.fori_loop(0, NX, project, 0)

    def s_copy(target, where):
        return pltpu.make_async_remote_copy(
            src_ref=sigmsg.at[target],
            dst_ref=xs.at[q],
            send_sem=bulk_send.at[1],
            recv_sem=bulk_recv.at[1],
            device_id=where,
            device_id_type=MESH,
        )

    def send_s(step, carry):
        target = lax.rem(q + step, Q)
        s_copy(target, {"y_lo": target // NZ, "z": lax.rem(target, NZ)}).start()
        return carry

    lax.fori_loop(1, Q, send_s, 0)
    own_s = pltpu.make_async_copy(sigmsg.at[q], xs.at[q], local_sem.at[3])
    own_s.start()

    gates = []
    for step in (1, 3, 2):
        copy = pltpu.make_async_remote_copy(
            src_ref=gmsg.at[wrap(x + step, NX)],
            dst_ref=gbuf.at[x],
            send_sem=g_send.at[step - 1],
            recv_sem=g_recv.at[3 - step],
            device_id=at_x(step),
            device_id_type=MESH,
        )
        copy.start()
        gates.append(copy)
    own_g = pltpu.make_async_copy(gmsg.at[x], gbuf.at[x], local_sem.at[4])
    own_g.start()

    def bulk_wait(index, src, dst):
        copy = pltpu.make_async_remote_copy(
            src_ref=src,
            dst_ref=dst,
            send_sem=bulk_send.at[index],
            recv_sem=bulk_recv.at[index],
            device_id=over_core,
            device_id_type=MESH,
        )
        copy.wait_send()
        copy.wait_recv()

    own_h.wait()
    bulk_wait(0, hmsg.at[pl.ds(0, NS - 1)], hbuf.at[:, pl.ds(0, (NS - 1) * 2 * CB)])
    hre[...] = hbuf[0].astype(F32)
    him[...] = hbuf[1].astype(F32)

    own_s.wait()
    bulk_wait(1, sigmsg.at[pl.ds(0, Q - 1)], xs.at[pl.ds(0, Q - 1)])
    xf[...] = xs[...].reshape(N1 * CB, N1).astype(F32)

    tc, ts = tc_ref[...], ts_ref[...]
    for c in range(CB):
        rows = pl.ds(c, N1, stride=CB)
        value = xf[rows, :].astype(BF16)
        step1 = dot(first_ref[...], jnp.concatenate([value, value], 0))
        re, im = step1[:N1], step1[N1:]
        turned = jnp.concatenate([re * tc + im * ts, im * tc - re * ts], 1)
        spectrum = three_pass(dot_nt, forward_ref[...], turned)
        re, im = spectrum[:N1], spectrum[N1:]
        fr, fi = hre[rows, :], him[rows, :]
        filtered = jnp.concatenate([fr * re - fi * im, fr * im + fi * re], 0)
        step3 = three_pass(dot, back_ref[...], filtered)
        re, im = step3[:N1], step3[N1:]
        turned = jnp.concatenate([re * tc - im * ts, im * tc + re * ts], 1)
        yf[rows, :] = three_pass(dot_nt, last_ref[...], turned)
    ybf[...] = yf[...].astype(BF16)

    def y_copy(s, where):
        return pltpu.make_async_remote_copy(
            src_ref=ybf.at[pl.ds(pl.multiple_of(s * 2 * CB, 2 * CB), 2 * CB)],
            dst_ref=ybuf.at[me_m],
            send_sem=bulk_send.at[2],
            recv_sem=bulk_recv.at[2],
            device_id=where,
            device_id_type=MESH,
        )

    def send_y(step, carry):
        _, s, where = peer(step)
        y_copy(s, where).start()
        return carry

    lax.fori_loop(1, NS, send_y, 0)
    own_y = pltpu.make_async_copy(ybf.at[own_rows], ybuf.at[me_m], local_sem.at[5])
    own_y.start()
    own_g.wait()
    for copy in gates:
        copy.wait()
    own_y.wait()
    bulk_wait(2, ybf.at[pl.ds(0, (NS - 1) * 2 * CB)], ybuf.at[pl.ds(0, NS - 1)])

    for chunk in range(NX):
        value = ybuf[chunk * Q : (chunk + 1) * Q].astype(F32)
        for i in range(2):
            block = value[:, i * CB : (i + 1) * CB].reshape(LANES, N1).T
            gate = gbuf[chunk, i * N1 : (i + 1) * N1, :].astype(F32)
            out_ref[i * N1 : (i + 1) * N1, chunk * LANES : (chunk + 1) * LANES] = (
                gate * block
            ).astype(BF16)

    for _, copy in started:
        copy.wait_send()


def shards(features, w_in, filter_real, filter_imag, skip_gain):
    d_rows, _, width = w_in.shape
    slices = w_in.reshape(d_rows, 3, NX, LANES).transpose(2, 0, 1, 3).reshape(NX, d_rows, COLS)
    consts = [jnp.asarray(table) for table in tables()]
    vmem = pl.BlockSpec(memory_space=pltpu.VMEM)
    hbm = pl.BlockSpec(memory_space=pl.ANY)
    dma = pltpu.SemaphoreType.DMA
    return pl.pallas_call(
        kernel,
        out_shape=jax.ShapeDtypeStruct((ROWS, width), BF16),
        in_specs=[hbm, hbm] + [vmem] * 9,
        out_specs=vmem,
        scratch_shapes=[
            pltpu.VMEM((NX, YH * NC, ROWS, DBLK), BF16),
            pltpu.VMEM((Q, WROWS, COLS), BF16),
            pltpu.VMEM((NS, 2, 2 * CB, N1), BF16),
            pltpu.VMEM((2, N1 * CB, N1), BF16),
            pltpu.VMEM((Q, 8 * CB, N1), BF16),
            pltpu.VMEM((Q, 8 * CB, N1), BF16),
            pltpu.VMEM((NX, ROWS, LANES), BF16),
            pltpu.VMEM((NX, ROWS, LANES), BF16),
            pltpu.VMEM((N1 * CB, N1), BF16),
            pltpu.VMEM((NS, 2 * CB, N1), BF16),
            pltpu.VMEM((N1 * CB, N1), F32),
            pltpu.VMEM((N1 * CB, N1), F32),
            pltpu.VMEM((N1 * CB, N1), F32),
            pltpu.VMEM((N1 * CB, N1), F32),
            dma((40,)),
            dma((32,)),
            dma((20,)),
            dma((3,)),
            dma((16,)),
            dma((3,)),
            dma((3,)),
            dma((3,)),
            dma((3,)),
            dma((6,)),
        ],
        compiler_params=pltpu.CompilerParams(
            collective_id=0, has_side_effects=True, vmem_limit_bytes=48 * 1024 * 1024
        ),
    )(features, slices, filter_real, filter_imag, skip_gain[None, :], *consts)


def solution(mesh):
    fine = Mesh(
        mesh.devices.reshape(YL, NZ, NX, YH, NC), ("y_lo", "z", "x", "y_hi", "core")
    )
    seq, chan = ("y_lo", "z", "x"), ("y_hi", "core")
    placed = (P(seq, chan), P(seq, None, chan), P(seq, chan), P(seq, chan), P(chan))
    return jax.shard_map(
        shards, mesh=fine, in_specs=placed, out_specs=P(seq, chan), check_vma=False
    )
```

```python
import functools

import jax
import jax.numpy as jnp
import numpy as np
from jax import lax
from jax.experimental import pallas as pl
from jax.experimental.pallas import tpu as pltpu
from jax.sharding import Mesh
from jax.sharding import PartitionSpec as P

MESH = pl.DeviceIdType.MESH
F32 = jnp.float32
BF16 = jnp.bfloat16

YL, NZ, NX, YH, NC = 2, 8, 4, 2, 2
NS = YL * NZ * NX
Q = YL * NZ
ROWS = 256
HALF = ROWS // 2
DBLK = 1024
LANES = 128
CB = 8
N1 = 128
WROWS = 64 * NX
COLS = 3 * LANES


def split16(table):
    high = table.astype(BF16)
    return high, (table - high.astype(F32)).astype(BF16)


def tables():
    index = np.arange(N1)
    angle = 2.0 * np.pi * ((index[:, None] * index[None, :]) % N1) / N1
    cos, sin = np.cos(angle), np.sin(angle)
    twist = 2.0 * np.pi * (index[:, None] * index[None, :]) / (N1 * N1)

    def pair(table):
        high = table.astype(np.float32).astype(jnp.bfloat16)
        low = (table - high.astype(np.float64)).astype(np.float32).astype(jnp.bfloat16)
        return high, low

    first = pair(np.concatenate([cos, -sin], 0))
    first = np.concatenate(first, 1)
    forward = np.concatenate(pair(np.block([[cos, sin], [-sin, cos]])), 0)
    back = np.concatenate(pair(np.block([[cos, -sin], [sin, cos]])), 0)
    last = np.concatenate(pair(np.concatenate([cos, -sin], 1) / (N1 * N1)), 0)
    twist = np.stack([np.cos(twist), np.sin(twist)]).astype(np.float32)
    return np.concatenate([first, forward, back, last], 0), twist


def dot(a, b):
    return jnp.dot(a, b, preferred_element_type=F32)


def dot_nt(a, b):
    return lax.dot_general(a, b, (((1,), (1,)), ((), ())), preferred_element_type=F32)


def three_pass(product, stacked, value):
    m = stacked.shape[0] // 2
    high, low = split16(value)
    both = product(stacked, high)
    return both[:m] + both[m:] + product(stacked[:m], low)


def kernel(
    feat_ref,
    w_ref,
    fre_hbm,
    fim_hbm,
    skip_hbm,
    dft_hbm,
    twist_hbm,
    out_ref,
    feat,
    wbuf,
    hmsg,
    hbuf,
    sigmsg,
    xs,
    gmsg,
    gbuf,
    ybf,
    ybuf,
    xf,
    yf,
    hre,
    him,
    fre_ref,
    fim_ref,
    skip_ref,
    dft_ref,
    twist_ref,
    f_send,
    f_recv,
    w_send,
    ws_recv,
    w_recv,
    g_send,
    g_recv,
    bulk_send,
    bulk_recv,
    local_sem,
    in_sem,
    own_w_sem,
):
    yl = lax.axis_index("y_lo")
    z = lax.axis_index("z")
    x = lax.axis_index("x")
    yh = lax.axis_index("y_hi")
    core = lax.axis_index("core")
    q = yl * NZ + z
    me_s = q * NX + x
    me_m = x * Q + q

    def wrap(value, count):
        return lax.rem(value + count, count)

    def at_x(step):
        return {"x": wrap(x + step, NX)}

    def at_z(step):
        return {"z": wrap(z + step, NZ)}

    over_yl, over_yh, over_core = {"y_lo": 1 - yl}, {"y_hi": 1 - yh}, {"core": 1 - core}

    def peer(step):
        m = lax.rem(me_m + step, NS)
        px, pq = m // Q, lax.rem(m, Q)
        return m, pq * NX + px, {"x": px, "y_lo": pq // NZ, "z": lax.rem(pq, NZ)}

    fetches = [
        pltpu.make_async_copy(src, dst, in_sem.at[index])
        for index, (src, dst) in enumerate(
            (
                (fre_hbm, fre_ref),
                (fim_hbm, fim_ref),
                (skip_hbm, skip_ref),
                (dft_hbm, dft_ref),
                (twist_hbm, twist_ref),
            )
        )
    ]
    for fetch in fetches:
        fetch.start()

    barrier = pltpu.get_barrier_semaphore()

    for where in (at_x(1),at_x(2),at_x(-1),at_z(1),at_z(-1),over_yl):
        pl.semaphore_signal(barrier, inc=1, device_id=where, device_id_type=MESH)
    pl.semaphore_signal(barrier, inc=1, device_id=over_yh, device_id_type=MESH)
    pl.semaphore_signal(barrier, inc=1, device_id=over_core, device_id_type=MESH)
    pl.semaphore_wait(barrier, 8)

    started = []

    def w_block(dz, dyl):
        return wbuf.at[(yl if dyl == 0 else 1 - yl) * NZ + wrap(z + dz, NZ)]

    def w_go(src, dst, recv_sem, where):
        index = len([1 for kind, _ in started if kind == "w"])
        copy = pltpu.make_async_remote_copy(
            src_ref=src,
            dst_ref=dst,
            send_sem=w_send.at[index],
            recv_sem=recv_sem,
            device_id=where,
            device_id_type=MESH,
        )
        copy.start()
        started.append(("w", copy))

    def w_await(dst, recv_sem):
        pltpu.make_async_remote_copy(
            src_ref=dst,
            dst_ref=dst,
            send_sem=w_send.at[0],
            recv_sem=recv_sem,
            device_id=over_core,
            device_id_type=MESH,
        ).wait_recv()

    def w_slot(dx, panel=None):
        rows = pl.ds(pl.multiple_of(wrap(x + dx, NX) * 64, 64), 64)
        if panel is None:
            return wbuf.at[q, rows]
        return wbuf.at[q, rows, pl.ds(panel * LANES, LANES)]

    def w_panel(dx, panel):
        lanes = pl.ds(pl.multiple_of(wrap(x + dx, NX) * LANES, LANES), LANES)
        return w_ref.at[panel, :, lanes]

    own_w = [
        pltpu.make_async_copy(w_panel(0, panel), w_slot(0, panel), own_w_sem.at[panel])
        for panel in range(3)
    ]
    for copy in own_w:
        copy.start()
    for step in (1, 3, 2):
        for panel in range(3):
            w_go(
                w_panel(step, panel),
                w_slot(0, panel),
                ws_recv.at[(3 - step) * 3 + panel],
                at_x(step),
            )

    def f_block(dx, dyh, dc, h):
        column = (yh if dyh == 0 else 1 - yh) * NC + (core if dc == 0 else 1 - core)
        return feat.at[wrap(x + dx, NX), column, pl.ds(h * HALF, HALF)]

    def f_sem(dx, dyh, dc, h):
        return f_recv.at[((dx % NX * 2 + dyh) * 2 + dc) * 2 + h]

    def f_go(src, block, here, where):
        dx, dyh, dc, h = here
        index = len([1 for kind, _ in started if kind == "f"])
        copy = pltpu.make_async_remote_copy(
            src_ref=src,
            dst_ref=block,
            send_sem=f_send.at[index],
            recv_sem=f_sem(dx, dyh, dc, h),
            device_id=where,
            device_id_type=MESH,
        )
        copy.start()
        started.append(("f", copy))

    def f_await(dx, dyh, dc, h):
        block = f_block(dx, dyh, dc, h)
        pltpu.make_async_remote_copy(
            src_ref=block,
            dst_ref=block,
            send_sem=f_send.at[0],
            recv_sem=f_sem(dx, dyh, dc, h),
            device_id=over_core,
            device_id_type=MESH,
        ).wait_recv()

    for h in range(2):
        src = feat_ref.at[pl.ds(h * HALF, HALF)]
        block = f_block(0, 0, 0, h)
        f_go(src, block, (3, 0, 0, h), at_x(1))
        f_go(src, block, (1, 0, 0, h), at_x(-1))
        f_go(src, block, (0, 1, 0, h), over_yh)
        f_go(src, block, (0, 0, 1, h), over_core)
    own_f = pltpu.make_async_copy(feat_ref, feat.at[x, yh * NC + core], local_sem.at[1])
    own_f.start()

    def forward_f(dx, dyh, h):
        f_await(dx, dyh, 0, h)
        block = f_block(dx, dyh, 0, h)
        if dx == 0:
            f_go(block, block, (3, dyh, 0, h), at_x(1))
            f_go(block, block, (1, dyh, 0, h), at_x(-1))
        if dx == 3 and h == 0:
            f_go(block, block, (2, dyh, 0, h), at_x(1))
        if dx == 1 and h == 1:
            f_go(block, block, (2, dyh, 0, h), at_x(-1))
        f_go(block, block, (dx, dyh, 1, h), over_core)

    def w_sem(dz, dyl):
        return w_recv.at[dz % NZ * 2 + dyl]

    def forward_w(dz, dyl):
        block = w_block(dz, dyl)
        if (dz, dyl) == (0, 0):
            for copy in own_w:
                copy.wait()
            for step in range(3):
                for panel in range(3):
                    w_await(w_slot(1 + step, panel), ws_recv.at[step * 3 + panel])
            w_go(block, block, w_sem(0, 1), over_yl)
        else:
            w_await(block, w_sem(dz, dyl))
        if -3 < dz <= 0 or (dz == -3 and dyl == 0):
            w_go(block, block, w_sem(dz - 1, dyl), at_z(1))
        if 0 <= dz < 3 or (dz == 3 and dyl == 1):
            w_go(block, block, w_sem(dz + 1, dyl), at_z(-1))

    def filter_rows(part, ref, chunk):
        lanes = pl.ds(pl.multiple_of(chunk * LANES, LANES), LANES)
        block = ref[:, lanes]
        if part == 0:
            block = block + skip_ref[:, lanes]
        turned = block.T
        parts = [turned[:, i * N1 : (i + 1) * N1].reshape(Q, 1, CB, N1) for i in range(2)]
        stacked = jnp.concatenate(parts, 1).reshape(Q, 2 * CB, N1)
        hmsg[pl.ds(chunk * Q, Q), part] = stacked.astype(BF16)

    def filter_chunk(chunk, carry):
        filter_rows(0, fre_ref, chunk)
        filter_rows(1, fim_ref, chunk)
        return carry

    for fetch in fetches[:3]:
        fetch.wait()
    lax.fori_loop(0, NX, filter_chunk, 0)
    own_rows = pl.ds(pl.multiple_of(me_s * 2 * CB, 2 * CB), 2 * CB)

    def h_copy(m, where):
        return pltpu.make_async_remote_copy(
            src_ref=hmsg.at[m],
            dst_ref=hbuf.at[:, own_rows],
            send_sem=bulk_send.at[0],
            recv_sem=bulk_recv.at[0],
            device_id=where,
            device_id_type=MESH,
        )

    def send_h(step, carry):
        m, _, where = peer(step)
        h_copy(m, where).start()
        return carry

    own_h = pltpu.make_async_copy(hmsg.at[me_m], hbuf.at[:, own_rows], local_sem.at[2])
    own_h.start()

    forward_w(0, 0)
    forward_w(0, 1)
    forward_f(3, 0, 0)
    forward_f(1, 0, 0)
    forward_w(-1, 0)
    forward_w(1, 0)
    forward_f(0, 1, 0)
    forward_f(3, 0, 1)
    forward_f(1, 0, 1)
    forward_w(-1, 1)
    forward_w(1, 1)
    forward_f(0, 1, 1)
    forward_w(-2, 0)
    forward_w(2, 0)
    forward_f(3, 1, 0)
    forward_f(1, 1, 0)
    forward_w(-2, 1)
    forward_w(2, 1)
    forward_f(3, 1, 1)
    forward_f(1, 1, 1)
    forward_w(-3, 0)
    forward_w(3, 0)
    forward_w(-3, 1)
    forward_w(3, 1)
    forward_f(2, 0, 0)
    forward_f(2, 0, 1)
    forward_f(2, 1, 0)
    forward_f(2, 1, 1)
    lax.fori_loop(1, NS, send_h, 0)
    w_await(w_block(-4, 0), w_sem(-4, 0))
    w_await(w_block(4, 1), w_sem(4, 1))
    own_f.wait()
    for dyh in (0, 1):
        for dx in range(NX):
            for h in range(2):
                f_await(dx, dyh, 1, h)

    def project(chunk, carry):
        total = dot(feat[chunk, 0], wbuf[0:4].reshape(DBLK, COLS))
        for j in range(1, 4):
            total = total + dot(feat[chunk, j], wbuf[4 * j : 4 * j + 4].reshape(DBLK, COLS))
        rounded = total.astype(BF16)
        signal = rounded[:, :LANES].astype(F32) * rounded[:, LANES : 2 * LANES].astype(F32)
        gmsg[chunk] = rounded[:, 2 * LANES :]
        turned = signal.T
        parts = [turned[:, i * N1 : (i + 1) * N1].reshape(Q, 1, CB, N1) for i in range(2)]
        stacked = jnp.concatenate(parts, 1).reshape(Q, 2 * CB, N1)
        sigmsg[:, pl.ds(pl.multiple_of(chunk * 16, 16), 16)] = stacked.astype(BF16)
        return carry

    lax.fori_loop(0, NX, project, 0)

    def s_copy(target, where):
        return pltpu.make_async_remote_copy(
            src_ref=sigmsg.at[target],
            dst_ref=xs.at[q],
            send_sem=bulk_send.at[1],
            recv_sem=bulk_recv.at[1],
            device_id=where,
            device_id_type=MESH,
        )

    def send_s(step, carry):
        target = lax.rem(q + step, Q)
        s_copy(target, {"y_lo": target // NZ, "z": lax.rem(target, NZ)}).start()
        return carry

    lax.fori_loop(1, Q, send_s, 0)
    own_s = pltpu.make_async_copy(sigmsg.at[q], xs.at[q], local_sem.at[3])
    own_s.start()

    gates = []
    for step in (1, 3, 2):
        copy = pltpu.make_async_remote_copy(
            src_ref=gmsg.at[wrap(x + step, NX)],
            dst_ref=gbuf.at[x],
            send_sem=g_send.at[step - 1],
            recv_sem=g_recv.at[3 - step],
            device_id=at_x(step),
            device_id_type=MESH,
        )
        copy.start()
        gates.append(copy)
    own_g = pltpu.make_async_copy(gmsg.at[x], gbuf.at[x], local_sem.at[4])
    own_g.start()

    def bulk_wait(index, src, dst):
        copy = pltpu.make_async_remote_copy(
            src_ref=src,
            dst_ref=dst,
            send_sem=bulk_send.at[index],
            recv_sem=bulk_recv.at[index],
            device_id=over_core,
            device_id_type=MESH,
        )
        copy.wait_send()
        copy.wait_recv()

    own_h.wait()
    bulk_wait(0, hmsg.at[pl.ds(0, NS - 1)], hbuf.at[:, pl.ds(0, (NS - 1) * 2 * CB)])
    hre[...] = hbuf[0].astype(F32)
    him[...] = hbuf[1].astype(F32)

    own_s.wait()
    bulk_wait(1, sigmsg.at[pl.ds(0, Q - 1)], xs.at[pl.ds(0, Q - 1)])
    xf[...] = xs[...].reshape(N1 * CB, N1).astype(F32)

    for fetch in fetches[3:]:
        fetch.wait()
    tc, ts = twist_ref[0], twist_ref[1]
    first, last = dft_ref[0:256], dft_ref[1280:1536]
    forward, back = dft_ref[256:768], dft_ref[768:1280]
    for c in range(CB):
        rows = pl.ds(c, N1, stride=CB)
        value = xf[rows, :].astype(BF16)
        step1 = dot(first, jnp.concatenate([value, value], 0))
        re, im = step1[:N1], step1[N1:]
        turned = jnp.concatenate([re * tc + im * ts, im * tc - re * ts], 1)
        spectrum = three_pass(dot_nt, forward, turned)
        re, im = spectrum[:N1], spectrum[N1:]
        fr, fi = hre[rows, :], him[rows, :]
        filtered = jnp.concatenate([fr * re - fi * im, fr * im + fi * re], 0)
        step3 = three_pass(dot, back, filtered)
        re, im = step3[:N1], step3[N1:]
        turned = jnp.concatenate([re * tc - im * ts, im * tc + re * ts], 1)
        yf[rows, :] = three_pass(dot_nt, last, turned)
    ybf[...] = yf[...].astype(BF16)

    def y_copy(s, where):
        return pltpu.make_async_remote_copy(
            src_ref=ybf.at[pl.ds(pl.multiple_of(s * 2 * CB, 2 * CB), 2 * CB)],
            dst_ref=ybuf.at[me_m],
            send_sem=bulk_send.at[2],
            recv_sem=bulk_recv.at[2],
            device_id=where,
            device_id_type=MESH,
        )

    def send_y(step, carry):
        _, s, where = peer(step)
        y_copy(s, where).start()
        return carry

    lax.fori_loop(1, NS, send_y, 0)
    own_y = pltpu.make_async_copy(ybf.at[own_rows], ybuf.at[me_m], local_sem.at[5])
    own_y.start()
    own_g.wait()
    for copy in gates:
        copy.wait()
    own_y.wait()
    bulk_wait(2, ybf.at[pl.ds(0, (NS - 1) * 2 * CB)], ybuf.at[pl.ds(0, NS - 1)])

    for chunk in range(NX):
        value = ybuf[chunk * Q : (chunk + 1) * Q].astype(F32)
        for i in range(2):
            block = value[:, i * CB : (i + 1) * CB].reshape(LANES, N1).T
            gate = gbuf[chunk, i * N1 : (i + 1) * N1, :].astype(F32)
            out_ref[i * N1 : (i + 1) * N1, chunk * LANES : (chunk + 1) * LANES] = (
                gate * block
            ).astype(BF16)

    for _, copy in started:
        copy.wait_send()


def shards(features, w_in, filter_real, filter_imag, skip_gain):
    d_rows, _, width = w_in.shape
    panels = w_in.transpose(1, 0, 2)
    consts = [jnp.asarray(table) for table in tables()]
    vmem = pl.BlockSpec(memory_space=pltpu.VMEM)
    hbm = pl.BlockSpec(memory_space=pltpu.HBM)
    dma = pltpu.SemaphoreType.DMA
    return pl.pallas_call(
        kernel,
        out_shape=jax.ShapeDtypeStruct((ROWS, width), BF16),
        in_specs=[hbm] * 7,
        out_specs=vmem,
        scratch_shapes=[
            pltpu.VMEM((NX, YH * NC, ROWS, DBLK), BF16),
            pltpu.VMEM((Q, WROWS, COLS), BF16),
            pltpu.VMEM((NS, 2, 2 * CB, N1), BF16),
            pltpu.VMEM((2, N1 * CB, N1), BF16),
            pltpu.VMEM((Q, 8 * CB, N1), BF16),
            pltpu.VMEM((Q, 8 * CB, N1), BF16),
            pltpu.VMEM((NX, ROWS, LANES), BF16),
            pltpu.VMEM((NX, ROWS, LANES), BF16),
            pltpu.VMEM((N1 * CB, N1), BF16),
            pltpu.VMEM((NS, 2 * CB, N1), BF16),
            pltpu.VMEM((N1 * CB, N1), F32),
            pltpu.VMEM((N1 * CB, N1), F32),
            pltpu.VMEM((N1 * CB, N1), F32),
            pltpu.VMEM((N1 * CB, N1), F32),
            pltpu.VMEM((ROWS, width), F32),
            pltpu.VMEM((ROWS, width), F32),
            pltpu.VMEM((1, width), F32),
            pltpu.VMEM((1536, 256), BF16),
            pltpu.VMEM((2, N1, N1), F32),
            dma((40,)),
            dma((32,)),
            dma((32,)),
            dma((9,)),
            dma((16,)),
            dma((3,)),
            dma((3,)),
            dma((3,)),
            dma((3,)),
            dma((6,)),
            dma((5,)),
            dma((3,)),
        ],
        compiler_params=pltpu.CompilerParams(
            collective_id=0, has_side_effects=True, vmem_limit_bytes=56 * 1024 * 1024
        ),
    )(features, panels, filter_real, filter_imag, skip_gain[None, :], *consts)


def solution(mesh):
    fine = Mesh(
        mesh.devices.reshape(YL, NZ, NX, YH, NC), ("y_lo", "z", "x", "y_hi", "core")
    )
    seq, chan = ("y_lo", "z", "x"), ("y_hi", "core")
    placed = (P(seq, chan), P(seq, None, chan), P(seq, chan), P(seq, chan), P(chan))
    return jax.shard_map(
        shards, mesh=fine, in_specs=placed, out_specs=P(seq, chan), check_vma=False
    )
```

```python
import functools

import jax
import jax.numpy as jnp
import numpy as np
from jax import lax
from jax.experimental import pallas as pl
from jax.experimental.pallas import tpu as pltpu
from jax.sharding import Mesh
from jax.sharding import PartitionSpec as P

MESH = pl.DeviceIdType.MESH
F32 = jnp.float32
BF16 = jnp.bfloat16

YL, NZ, NX, YH, NC = 2, 8, 4, 2, 2
NS = YL * NZ * NX
Q = YL * NZ
ROWS = 256
FPARTS = 4
FROWS = ROWS // FPARTS
DBLK = 1024
LANES = 128
GROUP = 8
CB = 8
N1 = 128
WROWS = 64 * NX
COLS = 3 * LANES


PLAN = (
    ("W", 0, 0, 0),
    ("F", 0, 0, 0),
    ("F", 0, 0, 1),
    ("F", 0, 0, 2),
    ("F", 0, 0, 3),
    ("W", 0, 0, 1),
    ("W", 0, 0, 3),
    ("W", -1, 0, 0),
    ("W", 1, 0, 0),
    ("W", 0, 0, 2),
    ("W", 0, 1, 0),
    ("F", 1, 0, 0),
    ("W", -1, 0, 1),
    ("W", 1, 0, 1),
    ("F", 3, 0, 0),
    ("h", 0, 0, 0),
    ("F", 0, 1, 0),
    ("W", -1, 0, 3),
    ("W", 1, 0, 3),
    ("W", -2, 0, 0),
    ("W", 2, 0, 0),
    ("F", 1, 0, 1),
    ("F", 3, 0, 1),
    ("W", -1, 0, 2),
    ("F", 0, 1, 1),
    ("W", 1, 0, 2),
    ("W", -1, 1, 0),
    ("W", 1, 1, 0),
    ("W", -2, 0, 1),
    ("W", 2, 0, 1),
    ("F", 1, 0, 2),
    ("F", 3, 0, 2),
    ("F", 0, 1, 2),
    ("W", -2, 0, 3),
    ("W", 2, 0, 3),
    ("W", -3, 0, 0),
    ("W", 3, 0, 0),
    ("F", 1, 0, 3),
    ("W", -2, 0, 2),
    ("W", 2, 0, 2),
    ("F", 3, 0, 3),
    ("F", 0, 1, 3),
    ("W", -2, 1, 0),
    ("W", 2, 1, 0),
    ("W", 0, 1, 1),
    ("W", -3, 0, 1),
    ("W", 3, 0, 1),
    ("W", 0, 1, 3),
    ("F", 1, 1, 0),
    ("F", 2, 0, 0),
    ("W", -3, 0, 3),
    ("W", 3, 0, 3),
    ("W", 0, 1, 2),
    ("W", -4, 0, 0),
    ("W", 3, 0, 2),
    ("W", -3, 0, 2),
    ("W", 3, 1, 0),
    ("F", 2, 0, 1),
    ("F", 3, 1, 0),
    ("W", -3, 1, 0),
    ("W", 1, 1, 1),
    ("W", -1, 1, 1),
    ("W", 1, 1, 3),
    ("F", 1, 1, 1),
    ("W", -4, 0, 1),
    ("W", 1, 1, 2),
    ("F", 3, 1, 1),
    ("W", -1, 1, 3),
    ("W", -4, 1, 0),
    ("W", -4, 0, 3),
    ("W", 2, 1, 1),
    ("F", 2, 1, 1),
    ("F", 1, 1, 2),
    ("F", 2, 0, 2),
    ("W", -1, 1, 2),
    ("W", 2, 1, 3),
    ("W", -4, 0, 2),
    ("W", 2, 1, 2),
    ("W", -2, 1, 1),
    ("W", 3, 1, 1),
    ("F", 2, 0, 3),
    ("F", 3, 1, 2),
    ("W", -2, 1, 3),
    ("W", 3, 1, 3),
    ("W", -2, 1, 2),
    ("W", 3, 1, 2),
    ("F", 1, 1, 3),
    ("W", -3, 1, 1),
    ("F", 3, 1, 3),
    ("W", -4, 1, 1),
    ("W", -3, 1, 3),
    ("W", -4, 1, 3),
    ("W", -3, 1, 2),
    ("F", 2, 1, 3),
    ("W", -4, 1, 2),
    ("F", 2, 1, 2),
    ("F", 2, 1, 0),
    ("H", 0, 1, 0),
)


def split16(table):
    high = table.astype(BF16)
    return high, (table - high.astype(F32)).astype(BF16)


def tables():
    index = np.arange(N1)
    angle = 2.0 * np.pi * ((index[:, None] * index[None, :]) % N1) / N1
    cos, sin = np.cos(angle), np.sin(angle)
    twist = 2.0 * np.pi * (index[:, None] * index[None, :]) / (N1 * N1)

    def pair(table):
        high = table.astype(np.float32).astype(jnp.bfloat16)
        low = (table - high.astype(np.float64)).astype(np.float32).astype(jnp.bfloat16)
        return high, low

    first = pair(np.concatenate([cos, -sin], 0))
    first = np.concatenate(first, 1)
    forward = np.concatenate(pair(np.block([[cos, sin], [-sin, cos]])), 0)
    back = np.concatenate(pair(np.block([[cos, -sin], [sin, cos]])), 0)
    last = np.concatenate(pair(np.concatenate([cos, -sin], 1) / (N1 * N1)), 0)
    twist = np.stack([np.cos(twist), np.sin(twist)]).astype(np.float32)
    return np.concatenate([first, forward, back, last], 0), twist


def dot(a, b):
    return jnp.dot(a, b, preferred_element_type=F32)


def dot_nt(a, b):
    return lax.dot_general(a, b, (((1,), (1,)), ((), ())), preferred_element_type=F32)


def three_pass(product, stacked, value):
    m = stacked.shape[0] // 2
    high, low = split16(value)
    both = product(stacked, high)
    return both[:m] + both[m:] + product(stacked[:m], low)


def kernel(
    feat_ref,
    w_ref,
    fre_hbm,
    fim_hbm,
    skip_hbm,
    dft_hbm,
    twist_hbm,
    out_ref,
    feat,
    wbuf,
    hmsg,
    hbuf,
    sigmsg,
    xs,
    gmsg,
    gbuf,
    ybf,
    ybuf,
    xf,
    yf,
    hre,
    him,
    fre_ref,
    fim_ref,
    skip_ref,
    dft_ref,
    twist_ref,
    f_send,
    f_recv,
    w_send,
    ws_recv,
    w_recv,
    g_send,
    g_recv,
    bulk_send,
    bulk_recv,
    local_sem,
    in_sem,
    own_w_sem,
):
    yl = lax.axis_index("y_lo")
    z = lax.axis_index("z")
    x = lax.axis_index("x")
    yh = lax.axis_index("y_hi")
    core = lax.axis_index("core")
    q = yl * NZ + z
    me_s = q * NX + x
    me_m = x * Q + q

    def wrap(value, count):
        return lax.rem(value + count, count)

    def at_x(step):
        return {"x": wrap(x + step, NX)}

    def at_z(step):
        return {"z": wrap(z + step, NZ)}

    over_yl, over_yh, over_core = {"y_lo": 1 - yl}, {"y_hi": 1 - yh}, {"core": 1 - core}

    def peer(step):
        m = lax.rem(me_m + step, NS)
        px, pq = m // Q, lax.rem(m, Q)
        return m, pq * NX + px, {"x": px, "y_lo": pq // NZ, "z": lax.rem(pq, NZ)}

    fetches = [
        pltpu.make_async_copy(src, dst, in_sem.at[index])
        for index, (src, dst) in enumerate(
            (
                (fre_hbm, fre_ref),
                (fim_hbm, fim_ref),
                (skip_hbm, skip_ref),
                (dft_hbm, dft_ref),
                (twist_hbm, twist_ref),
            )
        )
    ]
    for fetch in fetches:
        fetch.start()

    barrier = pltpu.get_barrier_semaphore()

    for where in (at_x(1),at_x(2),at_x(-1),at_z(1),at_z(-1),over_yl):
        pl.semaphore_signal(barrier, inc=1, device_id=where, device_id_type=MESH)
    pl.semaphore_signal(barrier, inc=1, device_id=over_yh, device_id_type=MESH)
    pl.semaphore_signal(barrier, inc=1, device_id=over_core, device_id_type=MESH)
    pl.semaphore_wait(barrier, 8)

    own_f = pltpu.make_async_copy(feat_ref, feat.at[x, yh * NC + core], local_sem.at[1])
    own_f.start()

    w_started, f_started = [], []

    def go(started, sems, src, dst, recv_sem, where):
        copy = pltpu.make_async_remote_copy(
            src_ref=src,
            dst_ref=dst,
            send_sem=sems.at[len(started)],
            recv_sem=recv_sem,
            device_id=where,
            device_id_type=MESH,
        )
        copy.start()
        started.append(copy)

    def arrived(dst, recv_sem):
        pltpu.make_async_remote_copy(
            src_ref=dst,
            dst_ref=dst,
            send_sem=w_send.at[0],
            recv_sem=recv_sem,
            device_id=over_core,
            device_id_type=MESH,
        ).wait_recv()

    def w_piece(dz, dyl, dx, panel=None):
        place = (yl if dyl == 0 else 1 - yl) * NZ + wrap(z + dz, NZ)
        rows = pl.ds(pl.multiple_of(wrap(x + dx, NX) * 64, 64), 64)
        if panel is None:
            return wbuf.at[place, rows]
        return wbuf.at[place, rows, pl.ds(panel * LANES, LANES)]

    def w_panel(dx, panel):
        lanes = pl.ds(pl.multiple_of(wrap(x + dx, NX) * LANES, LANES), LANES)
        return w_ref.at[panel, :, lanes]

    def w_go(here, there, where):
        dz, dyl, dx = there
        piece = w_piece(*here)
        recv_sem = w_recv.at[(dz % NZ * 2 + dyl) * NX + dx]
        go(w_started, w_send, piece, piece, recv_sem, where)

    def weights_arrived(dz, dyl, dx):
        here = (dz, dyl, dx)
        if here == (0, 0, 0):
            for copy in own_w:
                copy.wait()
        elif here[:2] == (0, 0):
            for panel in range(3):
                arrived(w_piece(0, 0, dx, panel), ws_recv.at[(dx - 1) * 3 + panel])
        else:
            arrived(w_piece(*here), w_recv.at[(dz % NZ * 2 + dyl) * NX + dx])
        if -3 < dz <= 0 or (dz == -3 and dyl == 0):
            w_go(here, (dz - 1, dyl, dx), at_z(1))
        if 0 <= dz < 3 or (dz == 3 and dyl == 1):
            w_go(here, (dz + 1, dyl, dx), at_z(-1))
        if here[:2] == (0, 0):
            w_go(here, (0, 1, dx), over_yl)

    own_w = [
        pltpu.make_async_copy(w_panel(0, panel), w_piece(0, 0, 0, panel), own_w_sem.at[panel])
        for panel in range(3)
    ]
    for copy in own_w:
        copy.start()
    for step in (1, 3, 2):
        for panel in range(3):
            go(
                w_started,
                w_send,
                w_panel(step, panel),
                w_piece(0, 0, 0, panel),
                ws_recv.at[(3 - step) * 3 + panel],
                at_x(step),
            )

    def f_piece(dx, dyh, dc, h):
        column = (yh if dyh == 0 else 1 - yh) * NC + (core if dc == 0 else 1 - core)
        return feat.at[wrap(x + dx, NX), column, pl.ds(h * FROWS, FROWS)]

    def f_sem(dx, dyh, dc, h):
        return f_recv.at[((dx % NX * 2 + dyh) * 2 + dc) * FPARTS + h]

    def features_arrived(dx, dyh, h):
        piece = f_piece(dx, dyh, 0, h)
        src = piece
        if (dx, dyh) == (0, 0):
            src = feat_ref.at[pl.ds(h * FROWS, FROWS)]
        else:
            arrived(piece, f_sem(dx, dyh, 0, h))

        def pass_on(there, where):
            go(f_started, f_send, src, piece, f_sem(*there), where)

        if dx == 0:
            pass_on((3, dyh, 0, h), at_x(1))
            pass_on((1, dyh, 0, h), at_x(-1))
        if (dx, dyh) == (0, 0):
            pass_on((0, 1, 0, h), over_yh)
        elif (dx, dyh) == (2, 0) and h % 2 == 1:
            pass_on((2, 1, 0, h), over_yh)
        elif dx in (1, 3):
            turn = (3, 1, 3, 1) if dyh == 0 else (3, 0, 1, 0)
            if turn[h] == dx:
                pass_on((2, dyh, 0, h), at_x(1 if dx == 3 else -1))
        pass_on((dx, dyh, 1, h), over_core)

    def filter_rows(part, ref, chunk):
        lanes = pl.ds(pl.multiple_of(chunk * LANES, LANES), LANES)
        block = ref[:, lanes]
        if part == 0:
            block = block + skip_ref[:, lanes]
        turned = block.T
        parts = [turned[:, i * N1 : (i + 1) * N1].reshape(Q, 1, CB, N1) for i in range(2)]
        stacked = jnp.concatenate(parts, 1).reshape(Q, 2 * CB, N1)
        hmsg[pl.ds(chunk * Q, Q), part] = stacked.astype(BF16)

    def filter_chunk(chunk, carry):
        filter_rows(0, fre_ref, chunk)
        filter_rows(1, fim_ref, chunk)
        return carry

    own_rows = pl.ds(pl.multiple_of(me_s * 2 * CB, 2 * CB), 2 * CB)

    def h_copy(m, where):
        return pltpu.make_async_remote_copy(
            src_ref=hmsg.at[m],
            dst_ref=hbuf.at[:, own_rows],
            send_sem=bulk_send.at[0],
            recv_sem=bulk_recv.at[0],
            device_id=where,
            device_id_type=MESH,
        )

    def send_h(step, carry):
        m, _, where = peer(step)
        h_copy(m, where).start()
        return carry

    own_h = pltpu.make_async_copy(hmsg.at[me_m], hbuf.at[:, own_rows], local_sem.at[2])
    for kind, one, two, three in PLAN:
        if kind == "W":
            weights_arrived(one, two, three)
        elif kind == "F":
            features_arrived(one, two, three)
        elif kind == "h":
            for fetch in fetches[:3]:
                fetch.wait()
            lax.fori_loop(0, NX, filter_chunk, 0)
            own_h.start()
        elif kind == "H":
            share = NS // two
            lax.fori_loop(max(1, one * share), (one + 1) * share, send_h, 0)
    own_f.wait()
    for dx in range(NX):
        for dyh in (0, 1):
            for h in range(FPARTS):
                arrived(f_piece(dx, dyh, 1, h), f_sem(dx, dyh, 1, h))

    def project(chunk, carry):
        total = dot(feat[chunk, 0], wbuf[0:4].reshape(DBLK, COLS))
        for j in range(1, 4):
            total = total + dot(feat[chunk, j], wbuf[4 * j : 4 * j + 4].reshape(DBLK, COLS))
        rounded = total.astype(BF16)
        signal = rounded[:, :LANES].astype(F32) * rounded[:, LANES : 2 * LANES].astype(F32)
        gmsg[chunk] = rounded[:, 2 * LANES :]
        turned = signal.T
        parts = [turned[:, i * N1 : (i + 1) * N1].reshape(Q, 1, CB, N1) for i in range(2)]
        stacked = jnp.concatenate(parts, 1).reshape(Q, 2 * CB, N1)
        sigmsg[:, pl.ds(pl.multiple_of(chunk * 16, 16), 16)] = stacked.astype(BF16)
        return carry

    lax.fori_loop(0, NX, project, 0)

    def s_copy(target, where):
        return pltpu.make_async_remote_copy(
            src_ref=sigmsg.at[target],
            dst_ref=xs.at[q],
            send_sem=bulk_send.at[1],
            recv_sem=bulk_recv.at[1],
            device_id=where,
            device_id_type=MESH,
        )

    def send_s(step, carry):
        target = lax.rem(q + step, Q)
        s_copy(target, {"y_lo": target // NZ, "z": lax.rem(target, NZ)}).start()
        return carry

    lax.fori_loop(1, Q, send_s, 0)
    own_s = pltpu.make_async_copy(sigmsg.at[q], xs.at[q], local_sem.at[3])
    own_s.start()

    gates = []
    for step in (1, 3, 2):
        copy = pltpu.make_async_remote_copy(
            src_ref=gmsg.at[wrap(x + step, NX)],
            dst_ref=gbuf.at[x],
            send_sem=g_send.at[step - 1],
            recv_sem=g_recv.at[3 - step],
            device_id=at_x(step),
            device_id_type=MESH,
        )
        copy.start()
        gates.append(copy)
    own_g = pltpu.make_async_copy(gmsg.at[x], gbuf.at[x], local_sem.at[4])
    own_g.start()

    def bulk_wait(index, src, dst):
        copy = pltpu.make_async_remote_copy(
            src_ref=src,
            dst_ref=dst,
            send_sem=bulk_send.at[index],
            recv_sem=bulk_recv.at[index],
            device_id=over_core,
            device_id_type=MESH,
        )
        copy.wait_send()
        copy.wait_recv()

    own_h.wait()
    bulk_wait(0, hmsg.at[pl.ds(0, NS - 1)], hbuf.at[:, pl.ds(0, (NS - 1) * 2 * CB)])
    hre[...] = hbuf[0].astype(F32)
    him[...] = hbuf[1].astype(F32)

    own_s.wait()
    bulk_wait(1, sigmsg.at[pl.ds(0, Q - 1)], xs.at[pl.ds(0, Q - 1)])
    xf[...] = xs[...].reshape(N1 * CB, N1).astype(F32)

    for fetch in fetches[3:]:
        fetch.wait()
    wide = GROUP * N1

    def tiled(table):
        return jnp.concatenate([table] * GROUP, 1)

    tc, ts = tiled(twist_ref[0]), tiled(twist_ref[1])
    first, last = dft_ref[0:256], dft_ref[1280:1536]
    forward, back = dft_ref[256:768], dft_ref[768:1280]

    def stack(re, im):
        return jnp.concatenate(
            [
                jnp.concatenate([t[:, g * N1 : (g + 1) * N1] for g in range(GROUP)], 0)
                for t in (re, im)
            ],
            1,
        )

    for base in range(0, CB, GROUP):
        rows = [pl.ds(base + g, N1, stride=CB) for g in range(GROUP)]

        def lanes(ref):
            return jnp.concatenate([ref[r, :] for r in rows], 1)

        value = lanes(xf).astype(BF16)
        step1 = dot(first, jnp.concatenate([value, value], 0))
        re, im = step1[:N1], step1[N1:]
        turned = stack(re * tc + im * ts, im * tc - re * ts)
        spectrum = three_pass(dot_nt, forward, turned)
        re, im = spectrum[:N1], spectrum[N1:]
        fr, fi = lanes(hre), lanes(him)
        filtered = jnp.concatenate([fr * re - fi * im, fr * im + fi * re], 0)
        step3 = three_pass(dot, back, filtered)
        re, im = step3[:N1], step3[N1:]
        turned = stack(re * tc - im * ts, im * tc + re * ts)
        result = three_pass(dot_nt, last, turned)
        for g in range(GROUP):
            yf[rows[g], :] = result[:, g * N1 : (g + 1) * N1]
    ybf[...] = yf[...].astype(BF16)

    def y_copy(s, where):
        return pltpu.make_async_remote_copy(
            src_ref=ybf.at[pl.ds(pl.multiple_of(s * 2 * CB, 2 * CB), 2 * CB)],
            dst_ref=ybuf.at[me_m],
            send_sem=bulk_send.at[2],
            recv_sem=bulk_recv.at[2],
            device_id=where,
            device_id_type=MESH,
        )

    def send_y(step, carry):
        _, s, where = peer(step)
        y_copy(s, where).start()
        return carry

    lax.fori_loop(1, NS, send_y, 0)
    own_y = pltpu.make_async_copy(ybf.at[own_rows], ybuf.at[me_m], local_sem.at[5])
    own_y.start()
    own_g.wait()
    for copy in gates:
        copy.wait()
    own_y.wait()
    bulk_wait(2, ybf.at[pl.ds(0, (NS - 1) * 2 * CB)], ybuf.at[pl.ds(0, NS - 1)])

    for chunk in range(NX):
        value = ybuf[chunk * Q : (chunk + 1) * Q].astype(F32)
        for i in range(2):
            block = value[:, i * CB : (i + 1) * CB].reshape(LANES, N1).T
            gate = gbuf[chunk, i * N1 : (i + 1) * N1, :].astype(F32)
            out_ref[i * N1 : (i + 1) * N1, chunk * LANES : (chunk + 1) * LANES] = (
                gate * block
            ).astype(BF16)

    for copy in w_started + f_started:
        copy.wait_send()


def shards(features, w_in, filter_real, filter_imag, skip_gain):
    d_rows, _, width = w_in.shape
    panels = w_in.transpose(1, 0, 2)
    consts = [jnp.asarray(table) for table in tables()]
    vmem = pl.BlockSpec(memory_space=pltpu.VMEM)
    hbm = pl.BlockSpec(memory_space=pltpu.HBM)
    dma = pltpu.SemaphoreType.DMA
    return pl.pallas_call(
        kernel,
        out_shape=jax.ShapeDtypeStruct((ROWS, width), BF16),
        in_specs=[hbm] * 7,
        out_specs=vmem,
        scratch_shapes=[
            pltpu.VMEM((NX, YH * NC, ROWS, DBLK), BF16),
            pltpu.VMEM((Q, WROWS, COLS), BF16),
            pltpu.VMEM((NS, 2, 2 * CB, N1), BF16),
            pltpu.VMEM((2, N1 * CB, N1), BF16),
            pltpu.VMEM((Q, 8 * CB, N1), BF16),
            pltpu.VMEM((Q, 8 * CB, N1), BF16),
            pltpu.VMEM((NX, ROWS, LANES), BF16),
            pltpu.VMEM((NX, ROWS, LANES), BF16),
            pltpu.VMEM((N1 * CB, N1), BF16),
            pltpu.VMEM((NS, 2 * CB, N1), BF16),
            pltpu.VMEM((N1 * CB, N1), F32),
            pltpu.VMEM((N1 * CB, N1), F32),
            pltpu.VMEM((N1 * CB, N1), F32),
            pltpu.VMEM((N1 * CB, N1), F32),
            pltpu.VMEM((ROWS, width), F32),
            pltpu.VMEM((ROWS, width), F32),
            pltpu.VMEM((1, width), F32),
            pltpu.VMEM((1536, 256), BF16),
            pltpu.VMEM((2, N1, N1), F32),
            dma((80,)),
            dma((16 * FPARTS,)),
            dma((80,)),
            dma((9,)),
            dma((64,)),
            dma((3,)),
            dma((3,)),
            dma((3,)),
            dma((3,)),
            dma((6,)),
            dma((5,)),
            dma((3,)),
        ],
        compiler_params=pltpu.CompilerParams(
            collective_id=0, has_side_effects=True, vmem_limit_bytes=56 * 1024 * 1024
        ),
    )(features, panels, filter_real, filter_imag, skip_gain[None, :], *consts)


def solution(mesh):
    fine = Mesh(
        mesh.devices.reshape(YL, NZ, NX, YH, NC), ("y_lo", "z", "x", "y_hi", "core")
    )
    seq, chan = ("y_lo", "z", "x"), ("y_hi", "core")
    placed = (P(seq, chan), P(seq, None, chan), P(seq, chan), P(seq, chan), P(chan))
    return jax.shard_map(
        shards, mesh=fine, in_specs=placed, out_specs=P(seq, chan), check_vma=False
    )
```

```python
import functools

import jax
import jax.numpy as jnp
import numpy as np
from jax import lax
from jax.experimental import pallas as pl
from jax.experimental.pallas import tpu as pltpu
from jax.sharding import Mesh
from jax.sharding import PartitionSpec as P

MESH = pl.DeviceIdType.MESH
F32 = jnp.float32
BF16 = jnp.bfloat16

YL, NZ, NX, YH, NC = 2, 8, 4, 2, 2
NS = YL * NZ * NX
Q = YL * NZ
ROWS = 256
FPARTS = 4
FROWS = ROWS // FPARTS
DBLK = 1024
LANES = 128
GROUP = 8
CB = 8
N1 = 128
WROWS = 64 * NX
COLS = 3 * LANES


PLAN = (
    ("W", 0, 0, 0),
    ("F", 0, 0, 0),
    ("Y", 0, 0, 0),
    ("F", 0, 0, 1),
    ("F", 0, 0, 2),
    ("F", 0, 0, 3),
    ("Y", 1, 0, 0),
    ("W", 0, 0, 1),
    ("W", 0, 0, 3),
    ("W", -1, 0, 0),
    ("W", 1, 0, 0),
    ("W", 0, 0, 2),
    ("W", 0, 1, 0),
    ("Y", 2, 0, 0),
    ("F", 1, 0, 0),
    ("h", 0, 0, 0),
    ("W", -1, 0, 1),
    ("W", 1, 0, 1),
    ("F", 3, 0, 0),
    ("F", 0, 1, 0),
    ("W", -1, 0, 3),
    ("W", 1, 0, 3),
    ("Y", 3, 0, 0),
    ("W", -2, 0, 0),
    ("W", 2, 0, 0),
    ("F", 1, 0, 1),
    ("F", 3, 0, 1),
    ("W", -1, 0, 2),
    ("F", 0, 1, 1),
    ("W", 1, 0, 2),
    ("W", -1, 1, 0),
    ("W", 0, 1, 1),
    ("W", 1, 1, 0),
    ("W", -2, 0, 1),
    ("W", 0, 1, 3),
    ("W", 2, 0, 1),
    ("F", 1, 0, 2),
    ("F", 3, 0, 2),
    ("W", -2, 0, 3),
    ("W", 0, 1, 2),
    ("W", 2, 0, 3),
    ("W", -3, 0, 0),
    ("W", 3, 0, 0),
    ("F", 1, 0, 3),
    ("W", -2, 0, 2),
    ("W", 2, 0, 2),
    ("F", 3, 0, 3),
    ("F", 0, 1, 2),
    ("W", -2, 1, 0),
    ("W", 1, 1, 1),
    ("W", -1, 1, 1),
    ("W", 2, 1, 0),
    ("F", 1, 1, 0),
    ("F", 2, 0, 0),
    ("W", -3, 0, 1),
    ("W", 1, 1, 3),
    ("F", 0, 1, 3),
    ("W", -1, 1, 3),
    ("W", 3, 0, 1),
    ("W", -3, 0, 3),
    ("W", 1, 1, 2),
    ("F", 2, 0, 1),
    ("F", 3, 1, 0),
    ("W", -1, 1, 2),
    ("P", 0, (0, -1, 1), 1),
    ("W", 3, 0, 3),
    ("W", -4, 0, 0),
    ("W", 3, 0, 2),
    ("F", 2, 1, 0),
    ("F", 1, 1, 1),
    ("W", -3, 0, 2),
    ("W", 2, 1, 1),
    ("F", 3, 1, 1),
    ("W", -3, 1, 0),
    ("W", 3, 1, 0),
    ("W", -2, 1, 1),
    ("W", 2, 1, 3),
    ("F", 2, 1, 1),
    ("F", 2, 0, 3),
    ("F", 2, 0, 2),
    ("W", -4, 0, 1),
    ("W", 2, 1, 2),
    ("W", -2, 1, 3),
    ("W", 3, 1, 1),
    ("W", -4, 0, 3),
    ("W", -4, 1, 0),
    ("F", 1, 1, 2),
    ("F", 3, 1, 2),
    ("W", -2, 1, 2),
    ("P", 0, (-2, 2), 0),
    ("W", 3, 1, 3),
    ("W", -4, 0, 2),
    ("W", 3, 1, 2),
    ("F", 2, 1, 3),
    ("F", 1, 1, 3),
    ("W", -3, 1, 1),
    ("W", -4, 1, 1),
    ("F", 3, 1, 3),
    ("H", 0, 1, 0),
    ("W", -3, 1, 3),
    ("W", -4, 1, 3),
    ("W", -3, 1, 2),
    ("F", 2, 1, 2),
    ("W", -4, 1, 2),
    ("P", 0, (-3, 3, -4), 2),
    ("P", 1, (0, -1, 1, -2, 2, -3, 3, -4), 3),
    ("P", 3, (0, -1, 1, -2, 2, -3, 3, -4), 3),
    ("P", 2, (0, -1, 1, -2, 2, -3, 3, -4), 3),
)


def split16(table):
    high = table.astype(BF16)
    return high, (table - high.astype(F32)).astype(BF16)


def tables():
    index = np.arange(N1)
    angle = 2.0 * np.pi * ((index[:, None] * index[None, :]) % N1) / N1
    cos, sin = np.cos(angle), np.sin(angle)
    twist = 2.0 * np.pi * (index[:, None] * index[None, :]) / (N1 * N1)

    def pair(table):
        high = table.astype(np.float32).astype(jnp.bfloat16)
        low = (table - high.astype(np.float64)).astype(np.float32).astype(jnp.bfloat16)
        return high, low

    first = pair(np.concatenate([cos, -sin], 0))
    first = np.concatenate(first, 1)
    forward = np.concatenate(pair(np.block([[cos, sin], [-sin, cos]])), 0)
    back = np.concatenate(pair(np.block([[cos, -sin], [sin, cos]])), 0)
    last = np.concatenate(pair(np.concatenate([cos, -sin], 1) / (N1 * N1)), 0)
    twist = np.stack([np.cos(twist), np.sin(twist)]).astype(np.float32)
    return np.concatenate([first, forward, back, last], 0), twist


def dot(a, b):
    return jnp.dot(a, b, preferred_element_type=F32)


def dot_nt(a, b):
    return lax.dot_general(a, b, (((1,), (1,)), ((), ())), preferred_element_type=F32)


def three_pass(product, stacked, value):
    m = stacked.shape[0] // 2
    high, low = split16(value)
    both = product(stacked, high)
    return both[:m] + both[m:] + product(stacked[:m], low)


def kernel(
    feat_ref,
    w_ref,
    fre_hbm,
    fim_hbm,
    skip_hbm,
    dft_hbm,
    twist_hbm,
    out_ref,
    feat,
    wbuf,
    hmsg,
    hbuf,
    sigmsg,
    xs,
    gmsg,
    gbuf,
    ybf,
    ybuf,
    xf,
    yf,
    hre,
    him,
    acc,
    fre_ref,
    fim_ref,
    skip_ref,
    dft_ref,
    twist_ref,
    f_send,
    f_recv,
    w_send,
    ws_recv,
    w_recv,
    g_send,
    g_recv,
    bulk_send,
    bulk_recv,
    local_sem,
    in_sem,
    own_w_sem,
):
    yl = lax.axis_index("y_lo")
    z = lax.axis_index("z")
    x = lax.axis_index("x")
    yh = lax.axis_index("y_hi")
    core = lax.axis_index("core")
    q = yl * NZ + z
    me_s = q * NX + x
    me_m = x * Q + q

    def wrap(value, count):
        return lax.rem(value + count, count)

    def at_x(step):
        return {"x": wrap(x + step, NX)}

    def at_z(step):
        return {"z": wrap(z + step, NZ)}

    over_yl, over_yh, over_core = {"y_lo": 1 - yl}, {"y_hi": 1 - yh}, {"core": 1 - core}

    def peer(step):
        m = lax.rem(me_m + step, NS)
        px, pq = m // Q, lax.rem(m, Q)
        return m, pq * NX + px, {"x": px, "y_lo": pq // NZ, "z": lax.rem(pq, NZ)}

    fetches = [
        pltpu.make_async_copy(src, dst, in_sem.at[index])
        for index, (src, dst) in enumerate(
            (
                (fre_hbm, fre_ref),
                (fim_hbm, fim_ref),
                (skip_hbm, skip_ref),
                (dft_hbm, dft_ref),
                (twist_hbm, twist_ref),
            )
        )
    ]
    for fetch in fetches:
        fetch.start()

    def w_piece(dz, dyl, dx, panel=None):
        place = (yl if dyl == 0 else 1 - yl) * NZ + wrap(z + dz, NZ)
        rows = pl.ds(pl.multiple_of(wrap(x + dx, NX) * 64, 64), 64)
        if panel is None:
            return wbuf.at[place, rows]
        return wbuf.at[place, rows, pl.ds(panel * LANES, LANES)]

    def w_panel(dx, panel):
        lanes = pl.ds(pl.multiple_of(wrap(x + dx, NX) * LANES, LANES), LANES)
        return w_ref.at[panel, :, lanes]

    own_w = [
        pltpu.make_async_copy(w_panel(0, panel), w_piece(0, 0, 0, panel), own_w_sem.at[panel])
        for panel in range(3)
    ]
    for copy in own_w:
        copy.start()
    own_f = pltpu.make_async_copy(feat_ref, feat.at[x, yh * NC + core], local_sem.at[1])
    own_f.start()

    barrier = pltpu.get_barrier_semaphore()

    for where in (at_x(1),at_x(2),at_x(-1),at_z(1),at_z(-1),over_yl):
        pl.semaphore_signal(barrier, inc=1, device_id=where, device_id_type=MESH)
    pl.semaphore_signal(barrier, inc=1, device_id=over_yh, device_id_type=MESH)
    pl.semaphore_signal(barrier, inc=1, device_id=over_core, device_id_type=MESH)
    pl.semaphore_wait(barrier, 8)

    w_started, f_started = [], []

    def go(started, sems, src, dst, recv_sem, where):
        copy = pltpu.make_async_remote_copy(
            src_ref=src,
            dst_ref=dst,
            send_sem=sems.at[len(started)],
            recv_sem=recv_sem,
            device_id=where,
            device_id_type=MESH,
        )
        copy.start()
        started.append(copy)

    def arrived(dst, recv_sem):
        pltpu.make_async_remote_copy(
            src_ref=dst,
            dst_ref=dst,
            send_sem=w_send.at[0],
            recv_sem=recv_sem,
            device_id=over_core,
            device_id_type=MESH,
        ).wait_recv()

    def w_go(here, there, where):
        dz, dyl, dx = there
        piece = w_piece(*here)
        recv_sem = w_recv.at[(dz % NZ * 2 + dyl) * NX + dx]
        go(w_started, w_send, piece, piece, recv_sem, where)

    def weights_arrived(dz, dyl, dx):
        here = (dz, dyl, dx)
        if here == (0, 0, 0):
            for copy in own_w:
                copy.wait()
        elif here[:2] == (0, 0):
            for panel in range(3):
                arrived(w_piece(0, 0, dx, panel), ws_recv.at[(dx - 1) * 3 + panel])
        else:
            arrived(w_piece(*here), w_recv.at[(dz % NZ * 2 + dyl) * NX + dx])
        if -3 < dz <= 0 or (dz == -3 and dyl == 0):
            w_go(here, (dz - 1, dyl, dx), at_z(1))
        if 0 <= dz < 3 or (dz == 3 and dyl == 1):
            w_go(here, (dz + 1, dyl, dx), at_z(-1))
        if here[:2] == (0, 0):
            w_go(here, (0, 1, dx), over_yl)

    for step in (1, 3, 2):
        for panel in range(3):
            go(
                w_started,
                w_send,
                w_panel(step, panel),
                w_piece(0, 0, 0, panel),
                ws_recv.at[(3 - step) * 3 + panel],
                at_x(step),
            )

    def f_piece(dx, dyh, dc, h):
        column = (yh if dyh == 0 else 1 - yh) * NC + (core if dc == 0 else 1 - core)
        return feat.at[wrap(x + dx, NX), column, pl.ds(h * FROWS, FROWS)]

    def f_sem(dx, dyh, dc, h):
        return f_recv.at[((dx % NX * 2 + dyh) * 2 + dc) * FPARTS + h]

    def features_arrived(dx, dyh, h):
        piece = f_piece(dx, dyh, 0, h)
        src = piece
        if (dx, dyh) == (0, 0):
            src = feat_ref.at[pl.ds(h * FROWS, FROWS)]
        else:
            arrived(piece, f_sem(dx, dyh, 0, h))

        def pass_on(there, where):
            go(f_started, f_send, src, piece, f_sem(*there), where)

        if dx == 0:
            pass_on((3, dyh, 0, h), at_x(1))
            pass_on((1, dyh, 0, h), at_x(-1))
        if (dx, dyh) == (2, 0) and h in (0, 1, 2, 3):
            pass_on((2, 1, 0, h), over_yh)
        elif dx in (1, 3):
            turn = (3, 1, 3, 1) if dyh == 0 else (0, 0, 0, 0)
            if turn[h] == dx:
                pass_on((2, dyh, 0, h), at_x(1 if dx == 3 else -1))
        pass_on((dx, dyh, 1, h), over_core)

    def features_over_yh(h):
        src = feat_ref.at[pl.ds(h * FROWS, FROWS)]
        go(f_started, f_send, src, f_piece(0, 0, 0, h), f_sem(0, 1, 0, h), over_yh)

    def filter_rows(part, ref, chunk):
        lanes = pl.ds(pl.multiple_of(chunk * LANES, LANES), LANES)
        block = ref[:, lanes]
        if part == 0:
            block = block + skip_ref[:, lanes]
        turned = block.T
        parts = [turned[:, i * N1 : (i + 1) * N1].reshape(Q, 1, CB, N1) for i in range(2)]
        stacked = jnp.concatenate(parts, 1).reshape(Q, 2 * CB, N1)
        hmsg[pl.ds(chunk * Q, Q), part] = stacked.astype(BF16)

    def filter_chunk(chunk, carry):
        filter_rows(0, fre_ref, chunk)
        filter_rows(1, fim_ref, chunk)
        return carry

    own_rows = pl.ds(pl.multiple_of(me_s * 2 * CB, 2 * CB), 2 * CB)

    def h_copy(m, where):
        return pltpu.make_async_remote_copy(
            src_ref=hmsg.at[m],
            dst_ref=hbuf.at[:, own_rows],
            send_sem=bulk_send.at[0],
            recv_sem=bulk_recv.at[0],
            device_id=where,
            device_id_type=MESH,
        )

    def send_h(step, carry):
        m, _, where = peer(step)
        h_copy(m, where).start()
        return carry

    def project(dx, dzs, ends):
        chunk = wrap(x + dx, NX)
        if ends % 2:
            if dx == 0:
                own_f.wait()
            for dyh in (0, 1):
                for h in range(FPARTS):
                    arrived(f_piece(dx, dyh, 1, h), f_sem(dx, dyh, 1, h))
        total = None if ends % 2 else acc[dx]
        for dz in dzs:
            pz = wrap(z + dz, NZ)
            lanes = pl.ds(pl.multiple_of(lax.rem(pz, 4) * WROWS, WROWS), WROWS)
            for pyl in range(YL):
                part = dot(feat[chunk, pyl * 2 + pz // 4, :, lanes], wbuf[pyl * NZ + pz])
                total = part if total is None else total + part
        if ends < 2:
            acc[dx] = total
            return
        rounded = total.astype(BF16)
        signal = rounded[:, :LANES].astype(F32) * rounded[:, LANES : 2 * LANES].astype(F32)
        gmsg[chunk] = rounded[:, 2 * LANES :]
        turned = signal.T
        parts = [turned[:, i * N1 : (i + 1) * N1].reshape(Q, 1, CB, N1) for i in range(2)]
        stacked = jnp.concatenate(parts, 1).reshape(Q, 2 * CB, N1)
        sigmsg[:, pl.ds(pl.multiple_of(chunk * 16, 16), 16)] = stacked.astype(BF16)

    own_h = pltpu.make_async_copy(hmsg.at[me_m], hbuf.at[:, own_rows], local_sem.at[2])
    for kind, one, two, three in PLAN:
        if kind == "W":
            weights_arrived(one, two, three)
        elif kind == "F":
            features_arrived(one, two, three)
        elif kind == "Y":
            features_over_yh(one)
        elif kind == "P":
            project(one, two, three)
        elif kind == "h":
            for fetch in fetches[:3]:
                fetch.wait()
            lax.fori_loop(0, NX, filter_chunk, 0)
            own_h.start()
        elif kind == "H":
            share = NS // two
            lax.fori_loop(max(1, one * share), (one + 1) * share, send_h, 0)

    def s_copy(target, where):
        return pltpu.make_async_remote_copy(
            src_ref=sigmsg.at[target],
            dst_ref=xs.at[q],
            send_sem=bulk_send.at[1],
            recv_sem=bulk_recv.at[1],
            device_id=where,
            device_id_type=MESH,
        )

    def send_s(step, carry):
        target = lax.rem(q + step, Q)
        s_copy(target, {"y_lo": target // NZ, "z": lax.rem(target, NZ)}).start()
        return carry

    lax.fori_loop(1, Q, send_s, 0)
    own_s = pltpu.make_async_copy(sigmsg.at[q], xs.at[q], local_sem.at[3])
    own_s.start()

    gates = []
    for step in (1, 3, 2):
        copy = pltpu.make_async_remote_copy(
            src_ref=gmsg.at[wrap(x + step, NX)],
            dst_ref=gbuf.at[x],
            send_sem=g_send.at[step - 1],
            recv_sem=g_recv.at[3 - step],
            device_id=at_x(step),
            device_id_type=MESH,
        )
        copy.start()
        gates.append(copy)
    own_g = pltpu.make_async_copy(gmsg.at[x], gbuf.at[x], local_sem.at[4])
    own_g.start()

    def bulk_wait(index, src, dst):
        copy = pltpu.make_async_remote_copy(
            src_ref=src,
            dst_ref=dst,
            send_sem=bulk_send.at[index],
            recv_sem=bulk_recv.at[index],
            device_id=over_core,
            device_id_type=MESH,
        )
        copy.wait_send()
        copy.wait_recv()

    own_h.wait()
    bulk_wait(0, hmsg.at[pl.ds(0, NS - 1)], hbuf.at[:, pl.ds(0, (NS - 1) * 2 * CB)])
    hre[...] = hbuf[0].astype(F32)
    him[...] = hbuf[1].astype(F32)

    own_s.wait()
    bulk_wait(1, sigmsg.at[pl.ds(0, Q - 1)], xs.at[pl.ds(0, Q - 1)])
    xf[...] = xs[...].reshape(N1 * CB, N1).astype(F32)

    for fetch in fetches[3:]:
        fetch.wait()
    wide = GROUP * N1

    def tiled(table):
        return jnp.concatenate([table] * GROUP, 1)

    tc, ts = tiled(twist_ref[0]), tiled(twist_ref[1])
    first, last = dft_ref[0:256], dft_ref[1280:1536]
    forward, back = dft_ref[256:768], dft_ref[768:1280]

    def stack(re, im):
        return jnp.concatenate(
            [
                jnp.concatenate([t[:, g * N1 : (g + 1) * N1] for g in range(GROUP)], 0)
                for t in (re, im)
            ],
            1,
        )

    for base in range(0, CB, GROUP):
        rows = [pl.ds(base + g, N1, stride=CB) for g in range(GROUP)]

        def lanes(ref):
            return jnp.concatenate([ref[r, :] for r in rows], 1)

        value = lanes(xf).astype(BF16)
        step1 = dot(first, jnp.concatenate([value, value], 0))
        re, im = step1[:N1], step1[N1:]
        turned = stack(re * tc + im * ts, im * tc - re * ts)
        spectrum = three_pass(dot_nt, forward, turned)
        re, im = spectrum[:N1], spectrum[N1:]
        fr, fi = lanes(hre), lanes(him)
        filtered = jnp.concatenate([fr * re - fi * im, fr * im + fi * re], 0)
        step3 = three_pass(dot, back, filtered)
        re, im = step3[:N1], step3[N1:]
        turned = stack(re * tc - im * ts, im * tc + re * ts)
        result = three_pass(dot_nt, last, turned)
        for g in range(GROUP):
            yf[rows[g], :] = result[:, g * N1 : (g + 1) * N1]
    ybf[...] = yf[...].astype(BF16)

    def y_copy(s, where):
        return pltpu.make_async_remote_copy(
            src_ref=ybf.at[pl.ds(pl.multiple_of(s * 2 * CB, 2 * CB), 2 * CB)],
            dst_ref=ybuf.at[me_m],
            send_sem=bulk_send.at[2],
            recv_sem=bulk_recv.at[2],
            device_id=where,
            device_id_type=MESH,
        )

    def send_y(step, carry):
        _, s, where = peer(step)
        y_copy(s, where).start()
        return carry

    lax.fori_loop(1, NS, send_y, 0)
    own_y = pltpu.make_async_copy(ybf.at[own_rows], ybuf.at[me_m], local_sem.at[5])
    own_y.start()
    for copy in w_started + f_started:
        copy.wait_send()
    own_g.wait()
    for copy in gates:
        copy.wait()
    own_y.wait()
    bulk_wait(2, ybf.at[pl.ds(0, (NS - 1) * 2 * CB)], ybuf.at[pl.ds(0, NS - 1)])

    for chunk in range(NX):
        value = ybuf[chunk * Q : (chunk + 1) * Q].astype(F32)
        for i in range(2):
            block = value[:, i * CB : (i + 1) * CB].reshape(LANES, N1).T
            gate = gbuf[chunk, i * N1 : (i + 1) * N1, :].astype(F32)
            out_ref[i * N1 : (i + 1) * N1, chunk * LANES : (chunk + 1) * LANES] = (
                gate * block
            ).astype(BF16)


def shards(features, w_in, filter_real, filter_imag, skip_gain):
    d_rows, _, width = w_in.shape
    panels = w_in.transpose(1, 0, 2)
    consts = [jnp.asarray(table) for table in tables()]
    vmem = pl.BlockSpec(memory_space=pltpu.VMEM)
    hbm = pl.BlockSpec(memory_space=pltpu.HBM)
    dma = pltpu.SemaphoreType.DMA
    return pl.pallas_call(
        kernel,
        out_shape=jax.ShapeDtypeStruct((ROWS, width), BF16),
        in_specs=[hbm] * 7,
        out_specs=vmem,
        scratch_shapes=[
            pltpu.VMEM((NX, YH * NC, ROWS, DBLK), BF16),
            pltpu.VMEM((Q, WROWS, COLS), BF16),
            pltpu.VMEM((NS, 2, 2 * CB, N1), BF16),
            pltpu.VMEM((2, N1 * CB, N1), BF16),
            pltpu.VMEM((Q, 8 * CB, N1), BF16),
            pltpu.VMEM((Q, 8 * CB, N1), BF16),
            pltpu.VMEM((NX, ROWS, LANES), BF16),
            pltpu.VMEM((NX, ROWS, LANES), BF16),
            pltpu.VMEM((N1 * CB, N1), BF16),
            pltpu.VMEM((NS, 2 * CB, N1), BF16),
            pltpu.VMEM((N1 * CB, N1), F32),
            pltpu.VMEM((N1 * CB, N1), F32),
            pltpu.VMEM((N1 * CB, N1), F32),
            pltpu.VMEM((N1 * CB, N1), F32),
            pltpu.VMEM((NX, ROWS, COLS), F32),
            pltpu.VMEM((ROWS, width), F32),
            pltpu.VMEM((ROWS, width), F32),
            pltpu.VMEM((1, width), F32),
            pltpu.VMEM((1536, 256), BF16),
            pltpu.VMEM((2, N1, N1), F32),
            dma((80,)),
            dma((16 * FPARTS,)),
            dma((80,)),
            dma((9,)),
            dma((64,)),
            dma((3,)),
            dma((3,)),
            dma((3,)),
            dma((3,)),
            dma((6,)),
            dma((5,)),
            dma((3,)),
        ],
        compiler_params=pltpu.CompilerParams(
            collective_id=0, has_side_effects=True, vmem_limit_bytes=56 * 1024 * 1024
        ),
    )(features, panels, filter_real, filter_imag, skip_gain[None, :], *consts)


def solution(mesh):
    fine = Mesh(
        mesh.devices.reshape(YL, NZ, NX, YH, NC), ("y_lo", "z", "x", "y_hi", "core")
    )
    seq, chan = ("y_lo", "z", "x"), ("y_hi", "core")
    placed = (P(seq, chan), P(seq, None, chan), P(seq, chan), P(seq, chan), P(chan))
    return jax.shard_map(
        shards, mesh=fine, in_specs=placed, out_specs=P(seq, chan), check_vma=False
    )
```

```python
import functools

import jax
import jax.numpy as jnp
import numpy as np
from jax import lax
from jax.experimental import pallas as pl
from jax.experimental.pallas import tpu as pltpu
from jax.sharding import Mesh
from jax.sharding import PartitionSpec as P

MESH = pl.DeviceIdType.MESH
F32 = jnp.float32
BF16 = jnp.bfloat16

YL, NZ, NX, YH, NC = 2, 8, 4, 2, 2
NS = YL * NZ * NX
Q = YL * NZ
ROWS = 256
FPARTS = 4
FROWS = ROWS // FPARTS
DBLK = 1024
LANES = 128
GROUP = 8
CB = 8
N1 = 128
WROWS = 64 * NX
COLS = 3 * LANES
FAR_OVER_Y = (0, 1, 2, 3)
FAR_TURN = (0, 0, 0, 0)
OVER_Y = (0,)


PLAN = (
    ("W", 0, 0, 0),
    ("F", 0, 0, 0),
    ("Y", 0, 0, 0),
    ("F", 0, 0, 1),
    ("F", 0, 0, 2),
    ("F", 0, 0, 3),
    ("Y", 1, 0, 0),
    ("h", 0, 0, 0),
    ("W", 0, 0, 1),
    ("W", 0, 0, 3),
    ("W", -1, 0, 0),
    ("W", 1, 0, 0),
    ("W", 0, 0, 2),
    ("W", 0, 1, 0),
    ("Y", 2, 0, 0),
    ("F", 1, 0, 0),
    ("W", -1, 0, 1),
    ("W", 1, 0, 1),
    ("F", 3, 0, 0),
    ("F", 0, 1, 0),
    ("W", -1, 0, 3),
    ("W", 1, 0, 3),
    ("Y", 3, 0, 0),
    ("W", -2, 0, 0),
    ("W", 2, 0, 0),
    ("F", 1, 0, 1),
    ("F", 3, 0, 1),
    ("W", -1, 0, 2),
    ("F", 0, 1, 1),
    ("W", 1, 0, 2),
    ("W", -1, 1, 0),
    ("W", 0, 1, 1),
    ("W", 1, 1, 0),
    ("W", -2, 0, 1),
    ("W", 0, 1, 3),
    ("W", 2, 0, 1),
    ("F", 1, 0, 2),
    ("F", 3, 0, 2),
    ("W", -2, 0, 3),
    ("W", 0, 1, 2),
    ("W", 2, 0, 3),
    ("W", -3, 0, 0),
    ("W", 3, 0, 0),
    ("F", 1, 0, 3),
    ("W", -2, 0, 2),
    ("W", 2, 0, 2),
    ("F", 3, 0, 3),
    ("F", 0, 1, 2),
    ("W", -2, 1, 0),
    ("W", 1, 1, 1),
    ("W", -1, 1, 1),
    ("W", 2, 1, 0),
    ("F", 1, 1, 0),
    ("F", 2, 0, 0),
    ("W", -3, 0, 1),
    ("W", 1, 1, 3),
    ("F", 0, 1, 3),
    ("W", -1, 1, 3),
    ("W", 3, 0, 1),
    ("W", -3, 0, 3),
    ("W", 1, 1, 2),
    ("F", 2, 0, 1),
    ("F", 3, 1, 0),
    ("W", -1, 1, 2),
    ("P", 0, (0, -1, 1), 1),
    ("W", 3, 0, 3),
    ("W", -4, 0, 0),
    ("W", 3, 0, 2),
    ("F", 2, 1, 0),
    ("F", 1, 1, 1),
    ("W", -3, 0, 2),
    ("W", 2, 1, 1),
    ("F", 3, 1, 1),
    ("W", -3, 1, 0),
    ("W", 3, 1, 0),
    ("W", -2, 1, 1),
    ("W", 2, 1, 3),
    ("F", 2, 1, 1),
    ("F", 2, 0, 3),
    ("F", 2, 0, 2),
    ("W", -4, 0, 1),
    ("W", 2, 1, 2),
    ("W", -2, 1, 3),
    ("W", 3, 1, 1),
    ("W", -4, 0, 3),
    ("W", -4, 1, 0),
    ("F", 1, 1, 2),
    ("F", 3, 1, 2),
    ("W", -2, 1, 2),
    ("P", 0, (-2, 2), 0),
    ("W", 3, 1, 3),
    ("W", -4, 0, 2),
    ("W", 3, 1, 2),
    ("H", 0, 1, 0),
    ("F", 2, 1, 3),
    ("F", 1, 1, 3),
    ("W", -3, 1, 1),
    ("W", -4, 1, 1),
    ("F", 3, 1, 3),
    ("W", -3, 1, 3),
    ("W", -4, 1, 3),
    ("W", -3, 1, 2),
    ("F", 2, 1, 2),
    ("W", -4, 1, 2),
    ("P", 0, (-3, 3, -4), 2),
    ("P", 1, (-2, 2, 0, -1, 1, -3, 3, -4), 3),
    ("P", 3, (-3, 3, -2, 2, 0, -1, 1, -4), 3),
    ("P", 2, (-4, -3, 3, -2, 2, 0, -1, 1), 3),
)


def split16(table):
    high = table.astype(BF16)
    return high, (table - high.astype(F32)).astype(BF16)


def tables():
    index = np.arange(N1)
    angle = 2.0 * np.pi * ((index[:, None] * index[None, :]) % N1) / N1
    cos, sin = np.cos(angle), np.sin(angle)
    twist = 2.0 * np.pi * (index[:, None] * index[None, :]) / (N1 * N1)

    def pair(table):
        high = table.astype(np.float32).astype(jnp.bfloat16)
        low = (table - high.astype(np.float64)).astype(np.float32).astype(jnp.bfloat16)
        return high, low

    first = pair(np.concatenate([cos, -sin], 0))
    first = np.concatenate(first, 1)
    forward = np.concatenate(pair(np.block([[cos, sin], [-sin, cos]])), 0)
    back = np.concatenate(pair(np.block([[cos, -sin], [sin, cos]])), 0)
    last = np.concatenate(pair(np.concatenate([cos, -sin], 1) / (N1 * N1)), 0)
    twist = np.stack([np.cos(twist), np.sin(twist)]).astype(np.float32)
    return np.concatenate([first, forward, back, last], 0), twist


def dot(a, b):
    return jnp.dot(a, b, preferred_element_type=F32)


def dot_nt(a, b):
    return lax.dot_general(a, b, (((1,), (1,)), ((), ())), preferred_element_type=F32)


def two_pass(product, stacked, value):
    m = stacked.shape[0] // 2
    both = product(stacked, value.astype(BF16))
    return both[:m] + both[m:]


def kernel(
    feat_ref,
    w_ref,
    fre_hbm,
    fim_hbm,
    skip_hbm,
    dft_hbm,
    twist_hbm,
    out_ref,
    feat,
    wbuf,
    hmsg,
    hbuf,
    sigmsg,
    xs,
    gmsg,
    gbuf,
    ybf,
    ybuf,
    xf,
    yf,
    hre,
    him,
    acc,
    fre_ref,
    fim_ref,
    skip_ref,
    dft_ref,
    twist_ref,
    f_send,
    f_recv,
    w_send,
    ws_recv,
    w_recv,
    g_send,
    g_recv,
    bulk_send,
    bulk_recv,
    local_sem,
    in_sem,
    own_w_sem,
):
    yl = lax.axis_index("y_lo")
    z = lax.axis_index("z")
    x = lax.axis_index("x")
    yh = lax.axis_index("y_hi")
    core = lax.axis_index("core")
    q = yl * NZ + z
    me_s = q * NX + x
    me_m = x * Q + q

    def wrap(value, count):
        return lax.rem(value + count, count)

    def at_x(step):
        return {"x": wrap(x + step, NX)}

    def at_z(step):
        return {"z": wrap(z + step, NZ)}

    over_yl, over_yh, over_core = {"y_lo": 1 - yl}, {"y_hi": 1 - yh}, {"core": 1 - core}

    def peer(step):
        m = lax.rem(me_m + step, NS)
        px, pq = m // Q, lax.rem(m, Q)
        return m, pq * NX + px, {"x": px, "y_lo": pq // NZ, "z": lax.rem(pq, NZ)}

    fetches = [
        pltpu.make_async_copy(src, dst, in_sem.at[index])
        for index, (src, dst) in enumerate(
            (
                (fre_hbm, fre_ref),
                (fim_hbm, fim_ref),
                (skip_hbm, skip_ref),
                (dft_hbm, dft_ref),
                (twist_hbm, twist_ref),
            )
        )
    ]
    for fetch in fetches:
        fetch.start()

    def w_piece(dz, dyl, dx, panel=None):
        place = (yl if dyl == 0 else 1 - yl) * NZ + wrap(z + dz, NZ)
        rows = pl.ds(pl.multiple_of(wrap(x + dx, NX) * 64, 64), 64)
        if panel is None:
            return wbuf.at[place, rows]
        return wbuf.at[place, rows, pl.ds(panel * LANES, LANES)]

    def w_panel(dx, panel):
        lanes = pl.ds(pl.multiple_of(wrap(x + dx, NX) * LANES, LANES), LANES)
        return w_ref.at[panel, :, lanes]

    own_w = [
        pltpu.make_async_copy(w_panel(0, panel), w_piece(0, 0, 0, panel), own_w_sem.at[panel])
        for panel in range(3)
    ]
    for copy in own_w:
        copy.start()
    own_f = pltpu.make_async_copy(feat_ref, feat.at[x, yh * NC + core], local_sem.at[1])
    own_f.start()

    barrier = pltpu.get_barrier_semaphore()

    for where in (at_x(1), at_x(2), at_x(-1), at_z(1), at_z(-1), over_yl):
        pl.semaphore_signal(barrier, inc=1, device_id=where, device_id_type=MESH)
    pl.semaphore_signal(barrier, inc=1, device_id=over_yh, device_id_type=MESH)
    pl.semaphore_signal(barrier, inc=1, device_id=over_core, device_id_type=MESH)
    pl.semaphore_wait(barrier, 8)

    w_started, f_started = [], []

    def go(started, sems, src, dst, recv_sem, where):
        copy = pltpu.make_async_remote_copy(
            src_ref=src,
            dst_ref=dst,
            send_sem=sems.at[len(started)],
            recv_sem=recv_sem,
            device_id=where,
            device_id_type=MESH,
        )
        copy.start()
        started.append(copy)

    def arrived(dst, recv_sem):
        pltpu.make_async_remote_copy(
            src_ref=dst,
            dst_ref=dst,
            send_sem=w_send.at[0],
            recv_sem=recv_sem,
            device_id=over_core,
            device_id_type=MESH,
        ).wait_recv()

    def w_go(here, there, where):
        dz, dyl, dx = there
        piece = w_piece(*here)
        recv_sem = w_recv.at[(dz % NZ * 2 + dyl) * NX + dx]
        go(w_started, w_send, piece, piece, recv_sem, where)

    def weights_arrived(dz, dyl, dx):
        here = (dz, dyl, dx)
        if here == (0, 0, 0):
            for copy in own_w:
                copy.wait()
        elif here[:2] == (0, 0):
            for panel in range(3):
                arrived(w_piece(0, 0, dx, panel), ws_recv.at[(dx - 1) * 3 + panel])
        else:
            arrived(w_piece(*here), w_recv.at[(dz % NZ * 2 + dyl) * NX + dx])
        left, right = (dz - 1) % NZ, (dz + 1) % NZ
        if (-3 < dz <= 0 or (dz == -3 and dyl == 0)) and not (dyl == 1 and left in OVER_Y):
            w_go(here, (dz - 1, dyl, dx), at_z(1))
        if (0 <= dz < 3 or (dz == 3 and dyl == 1)) and not (dyl == 1 and right in OVER_Y):
            w_go(here, (dz + 1, dyl, dx), at_z(-1))
        if dyl == 0 and dz % NZ in OVER_Y:
            w_go(here, (dz, 1, dx), over_yl)

    for step in (1, 3, 2):
        for panel in range(3):
            go(
                w_started,
                w_send,
                w_panel(step, panel),
                w_piece(0, 0, 0, panel),
                ws_recv.at[(3 - step) * 3 + panel],
                at_x(step),
            )

    def f_piece(dx, dyh, dc, h):
        column = (yh if dyh == 0 else 1 - yh) * NC + (core if dc == 0 else 1 - core)
        return feat.at[wrap(x + dx, NX), column, pl.ds(h * FROWS, FROWS)]

    def f_sem(dx, dyh, dc, h):
        return f_recv.at[((dx % NX * 2 + dyh) * 2 + dc) * FPARTS + h]

    def features_arrived(dx, dyh, h):
        piece = f_piece(dx, dyh, 0, h)
        src = piece
        if (dx, dyh) == (0, 0):
            src = feat_ref.at[pl.ds(h * FROWS, FROWS)]
        else:
            arrived(piece, f_sem(dx, dyh, 0, h))

        def pass_on(there, where):
            go(f_started, f_send, src, piece, f_sem(*there), where)

        if dx == 0:
            pass_on((3, dyh, 0, h), at_x(1))
            pass_on((1, dyh, 0, h), at_x(-1))
        if (dx, dyh) == (2, 0) and h in FAR_OVER_Y:
            pass_on((2, 1, 0, h), over_yh)
        elif dx in (1, 3):
            turn = (3, 1, 3, 1) if dyh == 0 else FAR_TURN
            if turn[h] == dx:
                pass_on((2, dyh, 0, h), at_x(1 if dx == 3 else -1))
        pass_on((dx, dyh, 1, h), over_core)

    def features_over_yh(h):
        src = feat_ref.at[pl.ds(h * FROWS, FROWS)]
        go(f_started, f_send, src, f_piece(0, 0, 0, h), f_sem(0, 1, 0, h), over_yh)

    def filter_rows(part, ref, chunk):
        lanes = pl.ds(pl.multiple_of(chunk * LANES, LANES), LANES)
        block = ref[:, lanes]
        if part == 0:
            block = block + skip_ref[:, lanes]
        turned = block.T
        parts = [turned[:, i * N1 : (i + 1) * N1].reshape(Q, 1, CB, N1) for i in range(2)]
        stacked = jnp.concatenate(parts, 1).reshape(Q, 2 * CB, N1)
        hmsg[pl.ds(chunk * Q, Q), part] = stacked.astype(BF16)

    def filter_chunk(chunk, carry):
        filter_rows(0, fre_ref, chunk)
        filter_rows(1, fim_ref, chunk)
        return carry

    own_rows = pl.ds(pl.multiple_of(me_s * 2 * CB, 2 * CB), 2 * CB)

    def h_copy(m, where):
        return pltpu.make_async_remote_copy(
            src_ref=hmsg.at[m],
            dst_ref=hbuf.at[:, own_rows],
            send_sem=bulk_send.at[0],
            recv_sem=bulk_recv.at[0],
            device_id=where,
            device_id_type=MESH,
        )

    def send_h(step, carry):
        m, _, where = peer(step)
        h_copy(m, where).start()
        return carry

    def project(dx, dzs, ends):
        chunk = wrap(x + dx, NX)
        if ends % 2:
            if dx == 0:
                own_f.wait()
            for dyh in (0, 1):
                for h in range(FPARTS):
                    arrived(f_piece(dx, dyh, 1, h), f_sem(dx, dyh, 1, h))
        total = None if ends % 2 else acc[dx]
        for dz in dzs:
            pz = wrap(z + dz, NZ)
            lanes = pl.ds(pl.multiple_of(lax.rem(pz, 4) * WROWS, WROWS), WROWS)
            for pyl in range(YL):
                part = dot(feat[chunk, pyl * 2 + pz // 4, :, lanes], wbuf[pyl * NZ + pz])
                total = part if total is None else total + part
        if ends < 2:
            acc[dx] = total
            return
        rounded = total.astype(BF16)
        signal = rounded[:, :LANES].astype(F32) * rounded[:, LANES : 2 * LANES].astype(F32)
        gmsg[chunk] = rounded[:, 2 * LANES :]
        turned = signal.T
        parts = [turned[:, i * N1 : (i + 1) * N1].reshape(Q, 1, CB, N1) for i in range(2)]
        stacked = jnp.concatenate(parts, 1).reshape(Q, 2 * CB, N1)
        sigmsg[:, pl.ds(pl.multiple_of(chunk * 16, 16), 16)] = stacked.astype(BF16)

    own_h = pltpu.make_async_copy(hmsg.at[me_m], hbuf.at[:, own_rows], local_sem.at[2])
    for kind, one, two, three in PLAN:
        if kind == "W":
            weights_arrived(one, two, three)
        elif kind == "F":
            features_arrived(one, two, three)
        elif kind == "Y":
            features_over_yh(one)
        elif kind == "P":
            project(one, two, three)
        elif kind == "h":
            for fetch in fetches[:3]:
                fetch.wait()
            lax.fori_loop(0, NX, filter_chunk, 0)
            own_h.start()
        elif kind == "H":
            share = NS // two
            lax.fori_loop(max(1, one * share), (one + 1) * share, send_h, 0)

    def s_copy(target, where):
        return pltpu.make_async_remote_copy(
            src_ref=sigmsg.at[target],
            dst_ref=xs.at[q],
            send_sem=bulk_send.at[1],
            recv_sem=bulk_recv.at[1],
            device_id=where,
            device_id_type=MESH,
        )

    def send_s(step, carry):
        target = lax.rem(q + step, Q)
        s_copy(target, {"y_lo": target // NZ, "z": lax.rem(target, NZ)}).start()
        return carry

    lax.fori_loop(1, Q, send_s, 0)
    own_s = pltpu.make_async_copy(sigmsg.at[q], xs.at[q], local_sem.at[3])
    own_s.start()

    gates = []
    for step in (1, 3, 2):
        copy = pltpu.make_async_remote_copy(
            src_ref=gmsg.at[wrap(x + step, NX)],
            dst_ref=gbuf.at[x],
            send_sem=g_send.at[step - 1],
            recv_sem=g_recv.at[3 - step],
            device_id=at_x(step),
            device_id_type=MESH,
        )
        copy.start()
        gates.append(copy)
    own_g = pltpu.make_async_copy(gmsg.at[x], gbuf.at[x], local_sem.at[4])
    own_g.start()

    def bulk_wait(index, src, dst):
        copy = pltpu.make_async_remote_copy(
            src_ref=src,
            dst_ref=dst,
            send_sem=bulk_send.at[index],
            recv_sem=bulk_recv.at[index],
            device_id=over_core,
            device_id_type=MESH,
        )
        copy.wait_send()
        copy.wait_recv()

    own_h.wait()
    bulk_wait(0, hmsg.at[pl.ds(0, NS - 1)], hbuf.at[:, pl.ds(0, (NS - 1) * 2 * CB)])
    hre[...] = hbuf[0].astype(F32)
    him[...] = hbuf[1].astype(F32)

    own_s.wait()
    bulk_wait(1, sigmsg.at[pl.ds(0, Q - 1)], xs.at[pl.ds(0, Q - 1)])
    xf[...] = xs[...].reshape(N1 * CB, N1).astype(F32)

    for fetch in fetches[3:]:
        fetch.wait()
    wide = GROUP * N1

    def tiled(table):
        return jnp.concatenate([table] * GROUP, 1)

    tc, ts = tiled(twist_ref[0]), tiled(twist_ref[1])
    first, last = dft_ref[0:256], dft_ref[1280:1536]
    forward, back = dft_ref[256:768], dft_ref[768:1280]

    def stack(re, im):
        return jnp.concatenate(
            [
                jnp.concatenate([t[:, g * N1 : (g + 1) * N1] for g in range(GROUP)], 0)
                for t in (re, im)
            ],
            1,
        )

    for base in range(0, CB, GROUP):
        rows = [pl.ds(base + g, N1, stride=CB) for g in range(GROUP)]

        def lanes(ref):
            return jnp.concatenate([ref[r, :] for r in rows], 1)

        value = lanes(xf).astype(BF16)
        step1 = dot(first, jnp.concatenate([value, value], 0))
        re, im = step1[:N1], step1[N1:]
        turned = stack(re * tc + im * ts, im * tc - re * ts)
        spectrum = two_pass(dot_nt, forward, turned)
        re, im = spectrum[:N1], spectrum[N1:]
        fr, fi = lanes(hre), lanes(him)
        filtered = jnp.concatenate([fr * re - fi * im, fr * im + fi * re], 0)
        step3 = two_pass(dot, back, filtered)
        re, im = step3[:N1], step3[N1:]
        turned = stack(re * tc - im * ts, im * tc + re * ts)
        result = two_pass(dot_nt, last, turned)
        for g in range(GROUP):
            yf[rows[g], :] = result[:, g * N1 : (g + 1) * N1]
    ybf[...] = yf[...].astype(BF16)

    def y_copy(s, where):
        return pltpu.make_async_remote_copy(
            src_ref=ybf.at[pl.ds(pl.multiple_of(s * 2 * CB, 2 * CB), 2 * CB)],
            dst_ref=ybuf.at[me_m],
            send_sem=bulk_send.at[2],
            recv_sem=bulk_recv.at[2],
            device_id=where,
            device_id_type=MESH,
        )

    def send_y(step, carry):
        _, s, where = peer(step)
        y_copy(s, where).start()
        return carry

    lax.fori_loop(1, NS, send_y, 0)
    own_y = pltpu.make_async_copy(ybf.at[own_rows], ybuf.at[me_m], local_sem.at[5])
    own_y.start()
    for copy in w_started + f_started:
        copy.wait_send()
    own_g.wait()
    for copy in gates:
        copy.wait()
    own_y.wait()
    bulk_wait(2, ybf.at[pl.ds(0, (NS - 1) * 2 * CB)], ybuf.at[pl.ds(0, NS - 1)])

    for chunk in range(NX):
        value = ybuf[chunk * Q : (chunk + 1) * Q].astype(F32)
        for i in range(2):
            block = value[:, i * CB : (i + 1) * CB].reshape(LANES, N1).T
            gate = gbuf[chunk, i * N1 : (i + 1) * N1, :].astype(F32)
            out_ref[i * N1 : (i + 1) * N1, chunk * LANES : (chunk + 1) * LANES] = (
                gate * block
            ).astype(BF16)


def shards(features, w_in, filter_real, filter_imag, skip_gain):
    d_rows, _, width = w_in.shape
    panels = w_in.transpose(1, 0, 2)
    consts = [jnp.asarray(table) for table in tables()]
    vmem = pl.BlockSpec(memory_space=pltpu.VMEM)
    hbm = pl.BlockSpec(memory_space=pltpu.HBM)
    dma = pltpu.SemaphoreType.DMA
    return pl.pallas_call(
        kernel,
        out_shape=jax.ShapeDtypeStruct((ROWS, width), BF16),
        in_specs=[hbm] * 7,
        out_specs=vmem,
        scratch_shapes=[
            pltpu.VMEM((NX, YH * NC, ROWS, DBLK), BF16),
            pltpu.VMEM((Q, WROWS, COLS), BF16),
            pltpu.VMEM((NS, 2, 2 * CB, N1), BF16),
            pltpu.VMEM((2, N1 * CB, N1), BF16),
            pltpu.VMEM((Q, 8 * CB, N1), BF16),
            pltpu.VMEM((Q, 8 * CB, N1), BF16),
            pltpu.VMEM((NX, ROWS, LANES), BF16),
            pltpu.VMEM((NX, ROWS, LANES), BF16),
            pltpu.VMEM((N1 * CB, N1), BF16),
            pltpu.VMEM((NS, 2 * CB, N1), BF16),
            pltpu.VMEM((N1 * CB, N1), F32),
            pltpu.VMEM((N1 * CB, N1), F32),
            pltpu.VMEM((N1 * CB, N1), F32),
            pltpu.VMEM((N1 * CB, N1), F32),
            pltpu.VMEM((NX, ROWS, COLS), F32),
            pltpu.VMEM((ROWS, width), F32),
            pltpu.VMEM((ROWS, width), F32),
            pltpu.VMEM((1, width), F32),
            pltpu.VMEM((1536, 256), BF16),
            pltpu.VMEM((2, N1, N1), F32),
            dma((80,)),
            dma((16 * FPARTS,)),
            dma((100,)),
            dma((9,)),
            dma((64,)),
            dma((3,)),
            dma((3,)),
            dma((3,)),
            dma((3,)),
            dma((6,)),
            dma((5,)),
            dma((3,)),
        ],
        compiler_params=pltpu.CompilerParams(
            collective_id=0, has_side_effects=True, vmem_limit_bytes=56 * 1024 * 1024
        ),
    )(features, panels, filter_real, filter_imag, skip_gain[None, :], *consts)


def solution(mesh):
    fine = Mesh(
        mesh.devices.reshape(YL, NZ, NX, YH, NC), ("y_lo", "z", "x", "y_hi", "core")
    )
    seq, chan = ("y_lo", "z", "x"), ("y_hi", "core")
    placed = (P(seq, chan), P(seq, None, chan), P(seq, chan), P(seq, chan), P(chan))
    return jax.shard_map(
        shards, mesh=fine, in_specs=placed, out_specs=P(seq, chan), check_vma=False
    )
```
